32 devices in a mesh: seq: 16 (over z, y, core), mp: 2 (over x).
Axes of the slice: x: 2, y: 2, z: 4, core: 2. Of those that a mesh axis runs over, the one named last changes fastest.
Arguments:
- tokens: bfloat16 [2048, 3584], P('seq'), may hold values from -6 to 6
- query_weight: bfloat16 [3584, 4096], P('seq', 'mp'), may hold values from -0.09375 to 0.09375
- key_weight: bfloat16 [3584, 4096], P('seq', 'mp'), may hold values from -0.09375 to 0.09375
- value_weight: bfloat16 [3584, 4096], P('seq', 'mp'), may hold values from -0.09375 to 0.09375
- adapter_down_maps: bfloat16 [3584, 128], replicated, may hold values from -0.09375 to 0.09375
- lifting_matrices: bfloat16 [2, 64, 4096], P(None, None, 'mp'), may hold values from -0.75 to 0.75
- decay_logarithms: float32 [32, 2048], P('mp', 'seq'), may hold values from -1 to 0, as said below
- output_gradient: bfloat16 [2048, 4096], P('seq', 'mp'), may hold values from -0.13183594 to 0.13183594
Outputs:
- grad_down: float32 [3584, 128], P(('seq', 'mp'))
- grad_up: float32 [2, 64, 4096], P(None, None, 'mp')
The draws below stay inside these ranges and needn't reach their ends.
Inputs may be any that keep to these rules, and one draw needn't show every extreme that they name: `decay_logarithms`: every entry is negative.
All inputs are finite; a program needn't handle non-finite values.
Results may differ from the reference program's by a relative error of at most 0.006.
Values may be sent and summed in bfloat16 or wider, within the bound.
A program may use at most 192 MiB of HBM per device.

```python
import math
import jax
import jax.numpy as jnp
from jax import lax

MODEL_WIDTH = 3584
HEADS = 32
HK = 128
ADAPTER_RANK = 64
TOK_DEV = 128
STREAM_LENGTH = 2048
HEAD_FEATURES = 4096


def draw_decay_logarithms(key, part):
    keys = jax.random.split(jax.random.fold_in(key, 7103), 8)
    slow_share = 0.5
    slow = jax.random.uniform(keys[0], (HEADS,), jnp.float32) < slow_share
    slow_rate = jnp.exp(jax.random.uniform(keys[1], (HEADS,), jnp.float32, math.log(0.02), math.log(0.2))) * 2.302585 / STREAM_LENGTH
    fast_rate = jnp.exp(jax.random.uniform(keys[2], (HEADS,), jnp.float32, math.log(1.0 / 50.0), math.log(1.0 / 30.0)))
    base = jnp.where(slow, slow_rate, fast_rate)
    nblocks = STREAM_LENGTH // TOK_DEV
    block_factor = jnp.exp(jax.random.uniform(keys[3], (HEADS, nblocks, 1), jnp.float32, math.log(0.4), 0.0))
    block_factor = jnp.broadcast_to(block_factor, (HEADS, nblocks, TOK_DEV)).reshape(HEADS, STREAM_LENGTH)
    token_factor = jnp.exp(jax.random.uniform(keys[4], (HEADS, STREAM_LENGTH), jnp.float32, math.log(0.5), math.log(1.5)))
    fading_speed = base[:, None] * block_factor * token_factor
    first_offset = jax.random.randint(keys[5], (HEADS, 1), 0, STREAM_LENGTH)
    second_offset = (first_offset + jax.random.randint(keys[7], (HEADS, 1), 1, STREAM_LENGTH)) % STREAM_LENGTH
    step_offsets = jnp.concatenate([first_offset, second_offset], axis=1)
    stack_level = jax.random.uniform(keys[6], (HEADS, 2), jnp.float32, math.log(0.5), math.log(0.8))
    spike_placement = jnp.arange(STREAM_LENGTH)[None, None, :] == step_offsets[:, :, None]
    spike_clusters = jnp.sum(jnp.where(spike_placement, stack_level[:, :, None], 0.0), axis=1)
    return (spike_clusters - fading_speed).astype(jnp.float32)


def level_of(rng, dims, cuts, smallest, high):
    factor_of, own = 1.0, jax.random.fold_in(rng, 6)
    for position, shards_of in cuts:
        draws = jnp.exp(jax.random.uniform(jax.random.fold_in(own, position), (shards_of,), jnp.float32, smallest / len(cuts), high / len(cuts)))
        factor_of = factor_of * jnp.repeat(draws, dims[position] // shards_of).reshape([-1 if axis == position else 1 for axis in range(len(dims))])
    return factor_of


def normal_values(key, shape, deviation, bound, shards=(), held_as=jnp.bfloat16):
    level = level_of(key, shape, shards, -0.22, 0.18) if shards else 1.0
    drawn = jax.random.normal(key, shape, jnp.float32) * deviation * level
    return jnp.minimum(jnp.maximum(drawn, -bound), bound).astype(held_as)


def setup_inputs(seed: int = 0) -> dict:
    seeds = jax.random.split(jax.random.key(seed), 9)
    return {
        "tokens": normal_values(seeds[0], (STREAM_LENGTH, MODEL_WIDTH), 1.0, 6.0, ((0, 16),)),
        "query_weight": normal_values(seeds[1], (MODEL_WIDTH, HEAD_FEATURES), MODEL_WIDTH ** -0.5, 0.09375, ((0, 16), (1, 2))),
        "key_weight": normal_values(seeds[2], (MODEL_WIDTH, HEAD_FEATURES), MODEL_WIDTH ** -0.5, 0.09375, ((0, 16), (1, 2))),
        "value_weight": normal_values(seeds[3], (MODEL_WIDTH, HEAD_FEATURES), MODEL_WIDTH ** -0.5, 0.09375, ((0, 16), (1, 2))),
        "adapter_down_maps": normal_values(seeds[4], (MODEL_WIDTH, 2 * ADAPTER_RANK), MODEL_WIDTH ** -0.5, 0.09375),
        "lifting_matrices": normal_values(seeds[5], (2, ADAPTER_RANK, HEAD_FEATURES), ADAPTER_RANK ** -0.5, 0.75, ((2, 2),)),
        "decay_logarithms": draw_decay_logarithms(jax.random.fold_in(seeds[8], 71), 0),
        "output_gradient": normal_values(seeds[7], (STREAM_LENGTH, HEAD_FEATURES), (STREAM_LENGTH ** -0.5), 0.13183594, ((0, 16), (1, 2))),
    }


adapter_scale = 2.0
eps_norm = 1e-06
exact_arithmetic = lax.Precision.HIGHEST

def split_heads(flat):
    return flat.reshape(flat.shape[0], HEADS, HK).transpose(1, 0, 2)

def join_heads(arr):
    return arr.transpose(1, 0, 2).reshape(arr.shape[1], HEADS * HK)

def round_half(arr):
    return lax.optimization_barrier(arr.astype(jnp.bfloat16)).astype(jnp.float32)

def decay_terms(decay_block):
    cumulative = jnp.cumsum(decay_block, axis=1)
    total = cumulative[:, -1]
    gain = jnp.exp(total)
    tail = jnp.exp(total[:, None] - cumulative)
    lead = jnp.exp(cumulative)
    length = decay_block.shape[1]
    causal = jnp.arange(length)[:, None] >= jnp.arange(length)[None, :]
    spread = cumulative[:, :, None] - cumulative[:, None, :]
    decay_mat = jnp.where(causal[None], jnp.exp(jnp.where(causal[None], spread, 0.0)), 0.0)
    return (gain, tail, lead, decay_mat)

def reference(tokens, query_weight, key_weight, value_weight, adapter_down_maps, lifting_matrices, decay_logarithms, output_gradient):
    blocks = jnp.arange(STREAM_LENGTH // TOK_DEV, dtype=jnp.int32)

    def inputs_of(index):
        start = (index * TOK_DEV).astype(jnp.int32)
        input_rows = lax.dynamic_slice_in_dim(tokens, start, TOK_DEV, 0)
        decay_block = lax.dynamic_slice_in_dim(decay_logarithms, start, TOK_DEV, 1)
        low_product = jnp.dot(input_rows, adapter_down_maps, preferred_element_type=jnp.float32).astype(jnp.bfloat16)
        return (start, input_rows, decay_block, low_product)

    def keys_values(input_rows, low_product):
        key_pre = jnp.dot(input_rows, key_weight, preferred_element_type=jnp.float32)
        value_before_norm = jnp.dot(input_rows, value_weight, preferred_element_type=jnp.float32) + adapter_scale * jnp.dot(low_product[:, ADAPTER_RANK:], lifting_matrices[1], preferred_element_type=jnp.float32)
        key_f = split_heads(jax.nn.silu(key_pre).astype(jnp.bfloat16)).astype(jnp.float32)
        value_f = split_heads(value_before_norm.astype(jnp.bfloat16)).astype(jnp.float32)
        return (key_f, value_f)

    def forward_step(state, index):
        start, input_rows, decay_block, low_product = inputs_of(index)
        key_f, value_f = keys_values(input_rows, low_product)
        gain, tail, lead, decay_mat = decay_terms(decay_block)
        local = jnp.einsum('hsi,hsj->hij', key_f * tail[:, :, None], value_f, precision=exact_arithmetic)
        return (gain[:, None, None] * state + local, state)
    zero_state = jnp.zeros((HEADS, HK, HK), jnp.float32)
    _, states = lax.scan(forward_step, zero_state, blocks)

    def backward_step(carry, inputs):
        later, grad_down, grad_up = carry
        index, state_in = inputs
        start, input_rows, decay_block, low_product = inputs_of(index)
        key_f, value_f = keys_values(input_rows, low_product)
        gain, tail, lead, decay_mat = decay_terms(decay_block)
        query_before_norm = jnp.dot(input_rows, query_weight, preferred_element_type=jnp.float32) + adapter_scale * jnp.dot(low_product[:, :ADAPTER_RANK], lifting_matrices[0], preferred_element_type=jnp.float32)
        query_f = split_heads(jax.nn.silu(query_before_norm).astype(jnp.bfloat16)).astype(jnp.float32)
        scores = jnp.einsum('htd,hsd->hts', query_f, key_f, precision=exact_arithmetic)
        mixed = round_half(scores * decay_mat)
        attn = jnp.einsum('hts,hsj->htj', mixed, value_f, precision=exact_arithmetic) + lead[:, :, None] * jnp.einsum('hti,hij->htj', query_f, state_in, precision=exact_arithmetic)
        rms = jnp.sqrt(lax.optimization_barrier(jnp.mean(attn * attn, axis=-1, keepdims=True)) + eps_norm)
        normed = attn / rms
        upstream = split_heads(lax.dynamic_slice_in_dim(output_gradient, start, TOK_DEV, 0).astype(jnp.float32))
        d_attn = (upstream - normed * lax.optimization_barrier(jnp.mean(upstream * normed, axis=-1, keepdims=True))) / rms
        d_attn_b = round_half(d_attn)
        carried = jnp.einsum('hti,htj->hij', query_f * lead[:, :, None], d_attn, precision=exact_arithmetic)
        d_mixed = round_half(jnp.einsum('htj,hsj->hts', d_attn_b, value_f, precision=exact_arithmetic) * decay_mat)
        d_query = jnp.einsum('hts,hsi->hti', d_mixed, key_f, precision=exact_arithmetic) + lead[:, :, None] * jnp.einsum('htj,hij->hti', d_attn, state_in, precision=exact_arithmetic)
        d_value = jnp.einsum('hts,htj->hsj', mixed, d_attn_b, precision=exact_arithmetic) + tail[:, :, None] * jnp.einsum('hsi,hij->hsj', key_f, later, precision=exact_arithmetic)
        sig = jax.nn.sigmoid(query_before_norm)
        query_pre_gradient = join_heads(d_query) * (sig * (1.0 + query_before_norm * (1.0 - sig)))
        value_flat_gradient = join_heads(d_value)
        low_product_float = low_product.astype(jnp.float32)
        up_products = jnp.stack([adapter_scale * jnp.dot(low_product_float[:, :ADAPTER_RANK].T, query_pre_gradient, precision=exact_arithmetic), adapter_scale * jnp.dot(low_product_float[:, ADAPTER_RANK:].T, value_flat_gradient, precision=exact_arithmetic)])
        low_gradient = adapter_scale * jnp.concatenate([jnp.dot(query_pre_gradient, lifting_matrices[0].astype(jnp.float32).T, precision=exact_arithmetic), jnp.dot(value_flat_gradient, lifting_matrices[1].astype(jnp.float32).T, precision=exact_arithmetic)], axis=1)
        down_terms = jnp.dot(input_rows.astype(jnp.float32).T, low_gradient, precision=exact_arithmetic)
        later_next = carried + gain[:, None, None] * later
        return ((later_next, grad_down + down_terms, grad_up + up_products), None)
    init = (zero_state, jnp.zeros((MODEL_WIDTH, 2 * ADAPTER_RANK), jnp.float32), jnp.zeros((2, ADAPTER_RANK, HEADS * HK), jnp.float32))
    (_, grad_down, grad_up), _ = lax.scan(backward_step, init, (blocks, states), reverse=True)
    return (grad_down, grad_up)
```

```python
import functools

import jax
import jax.numpy as jnp
from jax import lax
from jax.experimental import pallas as pl
from jax.experimental.pallas import tpu as pltpu
from jax.sharding import PartitionSpec as P

adapter_scale = 2.0
eps_norm = 1e-06
exact_arithmetic = lax.Precision.HIGHEST


def carried_in(value, axis, join, neutral, backward):
    count, mine = (lax.axis_size(axis), lax.axis_index(axis))
    pieces = jax.tree.map(lambda part: lax.all_gather(part, axis), value)
    if backward:
        pieces = jax.tree.map(lambda part: part[::-1], pieces)
        mine = count - 1 - mine
    so_far = jax.tree.map(
        lambda part, zero: jnp.full_like(part, 0) + jnp.asarray(zero, part.dtype), value, neutral
    )

    def hop(position, so_far):
        longer = join(so_far, jax.tree.map(lambda part: part[position], pieces))
        return jax.tree.map(lambda new, old: jnp.where(position < mine, new, old), longer, so_far)

    return lax.fori_loop(0, count - 1, hop, so_far)


def combine(earlier, later):
    return (earlier[0] * later[0], later[0][:, None, None] * earlier[1] + later[1])


def split_heads(flat, heads):
    return flat.reshape(flat.shape[0], heads, flat.shape[1] // heads).transpose(1, 0, 2)


def join_heads(arr):
    return arr.transpose(1, 0, 2).reshape(arr.shape[1], arr.shape[0] * arr.shape[2])


def on_device(
    tokens,
    query_weight,
    key_weight,
    value_weight,
    adapter_down_maps,
    lifting_matrices,
    decay_logarithms,
    output_gradient,
):
    length = tokens.shape[0]
    heads = decay_logarithms.shape[0]
    rank_index = lifting_matrices.shape[1]
    low_product = jnp.dot(tokens, adapter_down_maps, preferred_element_type=jnp.float32).astype(
        jnp.bfloat16
    )
    query_low_product = low_product[:, :rank_index]
    value_low_product = low_product[:, rank_index:]
    cumulative = jnp.cumsum(decay_logarithms, axis=1)
    total = cumulative[:, -1]
    gain = jnp.exp(total)
    tail = jnp.exp(total[:, None] - cumulative)
    lead = jnp.exp(cumulative)
    causal = jnp.arange(length)[:, None] >= jnp.arange(length)[None, :]
    spread = cumulative[:, :, None] - cumulative[:, None, :]
    decay_mat = jnp.where(causal[None], jnp.exp(jnp.where(causal[None], spread, 0.0)), 0.0)
    pieces = (
        lax.all_gather(query_weight, "seq", axis=0, tiled=True),
        lax.all_gather(key_weight, "seq", axis=0, tiled=True),
        lax.all_gather(value_weight, "seq", axis=0, tiled=True),
    )
    columns = tokens
    query_frozen_part, key_base, value_frozen_part = tuple(
        (jnp.dot(columns, piece, preferred_element_type=jnp.float32) for piece in pieces)
    )
    value_before_norm = value_frozen_part + adapter_scale * jnp.dot(
        value_low_product, lifting_matrices[1], preferred_element_type=jnp.float32
    )
    key_heads = split_heads(jax.nn.silu(key_base).astype(jnp.bfloat16), heads)
    value_heads = split_heads(value_before_norm.astype(jnp.bfloat16), heads)
    key_f = key_heads.astype(jnp.float32)
    local = jnp.einsum(
        "hsi,hsj->hij",
        key_f * tail[:, :, None],
        value_heads.astype(jnp.float32),
        precision=exact_arithmetic,
    )
    state_in = carried_in(
        (gain, local), "seq", combine, (jnp.ones_like(gain), jnp.zeros_like(local)), False
    )[1]
    key_heads, key_f, value_heads, state_in = (key_heads, key_f, value_heads, state_in)
    query_before_norm = query_frozen_part + adapter_scale * jnp.dot(
        query_low_product, lifting_matrices[0], preferred_element_type=jnp.float32
    )
    query_heads = split_heads(jax.nn.silu(query_before_norm).astype(jnp.bfloat16), heads)
    query_f = query_heads.astype(jnp.float32)
    scores = jnp.einsum("htd,hsd->hts", query_heads, key_heads, preferred_element_type=jnp.float32)
    mixed = (scores * decay_mat).astype(jnp.bfloat16)
    attn = jnp.einsum(
        "hts,hsj->htj", mixed, value_heads, preferred_element_type=jnp.float32
    ) + lead[:, :, None] * jnp.einsum("hti,hij->htj", query_f, state_in, precision=exact_arithmetic)
    rms = jnp.sqrt(jnp.mean(attn * attn, axis=-1, keepdims=True) + eps_norm)
    normed = attn / rms
    upstream = split_heads(output_gradient, heads).astype(jnp.float32)
    d_attn = (upstream - normed * jnp.mean(upstream * normed, axis=-1, keepdims=True)) / rms
    d_attn_b = d_attn.astype(jnp.bfloat16)
    carried = jnp.einsum(
        "hti,htj->hij", query_f * lead[:, :, None], d_attn, precision=exact_arithmetic
    )
    later = carried_in(
        (gain, carried), "seq", combine, (jnp.ones_like(gain), jnp.zeros_like(carried)), True
    )[1]
    d_mixed = (
        jnp.einsum("htj,hsj->hts", d_attn_b, value_heads, preferred_element_type=jnp.float32)
        * decay_mat
    ).astype(jnp.bfloat16)
    d_query = jnp.einsum(
        "hts,hsi->hti", d_mixed, key_heads, preferred_element_type=jnp.float32
    ) + lead[:, :, None] * jnp.einsum("htj,hij->hti", d_attn, state_in, precision=exact_arithmetic)
    d_value = jnp.einsum(
        "hts,htj->hsj", mixed, d_attn_b, preferred_element_type=jnp.float32
    ) + tail[:, :, None] * jnp.einsum("hsi,hij->hsj", key_f, later, precision=exact_arithmetic)
    sig = jax.nn.sigmoid(query_before_norm)
    query_pre_gradient = join_heads(d_query) * (sig * (1.0 + query_before_norm * (1.0 - sig)))
    value_flat_gradient = join_heads(d_value)
    low_product_float = low_product.astype(jnp.float32)
    up_products = jnp.stack(
        [
            adapter_scale
            * jnp.dot(
                low_product_float[:, :rank_index].T, query_pre_gradient, precision=exact_arithmetic
            ),
            adapter_scale
            * jnp.dot(
                low_product_float[:, rank_index:].T, value_flat_gradient, precision=exact_arithmetic
            ),
        ]
    )
    grad_up = lax.psum(up_products, "seq")
    low_gradient = adapter_scale * jnp.concatenate(
        [
            jnp.dot(
                query_pre_gradient,
                lifting_matrices[0].astype(jnp.float32).T,
                precision=exact_arithmetic,
            ),
            jnp.dot(
                value_flat_gradient,
                lifting_matrices[1].astype(jnp.float32).T,
                precision=exact_arithmetic,
            ),
        ],
        axis=1,
    )
    seq_count = lax.axis_size("seq")
    model_count = lax.axis_size("mp")
    own_rows = tokens.shape[1] // (seq_count * model_count)
    whole_low = lax.psum(low_gradient, "mp")
    grouped = tokens.reshape(length, seq_count, model_count, own_rows)
    mine = lax.dynamic_index_in_dim(grouped, lax.axis_index("mp"), 2, keepdims=False).reshape(
        length, seq_count * own_rows
    )
    columns = mine.astype(jnp.float32)
    grad_down = lax.psum_scatter(
        jnp.dot(columns.T, whole_low, precision=exact_arithmetic),
        "seq",
        scatter_dimension=0,
        tiled=True,
    )
    return (grad_down, grad_up)


def dot_f32(a, b, contract):
    return lax.dot_general(a, b, ((contract[:1], contract[1:]), ((), ())), preferred_element_type=jnp.float32)


def layer_kernel(
    rank,
    tokens_ref,
    weight_ref,
    lift_ref,
    cumulative_ref,
    upstream_ref,
    low_grad_ref,
    up_ref,
    state,
    low_all,
    key_all,
    carried_all,
    grads,
):
    step = pl.program_id(0)
    steps = pl.num_programs(0)
    length = tokens_ref.shape[0]
    size = state.shape[0]
    half = jnp.bfloat16

    def decays(block):
        row = jnp.broadcast_to(cumulative_ref[pl.ds(block, 1), :], (length, length))
        column = row.T
        last = row[:, length - 1 :]
        return row, column, jnp.broadcast_to(last, (length, length))

    @pl.when(step == 0)
    def _():
        state[...] = jnp.zeros_like(state)

    product = jnp.dot(tokens_ref[...], weight_ref[...], preferred_element_type=jnp.float32)
    low = product[:, 3 * size :].astype(half)
    lifted = jnp.dot(low, lift_ref[...], preferred_element_type=jnp.float32)
    query_pre = product[:, :size] + lifted[:, :size]
    key_pre = product[:, size : 2 * size]
    value = (product[:, 2 * size : 3 * size] + lifted[:, size:]).astype(half)
    sig = jax.nn.sigmoid(query_pre)
    query = (query_pre * sig).astype(half)
    key = (key_pre * jax.nn.sigmoid(key_pre)).astype(half)
    row, column, total = decays(step)
    causal = lax.broadcasted_iota(jnp.int32, (length, length), 0) >= lax.broadcasted_iota(
        jnp.int32, (length, length), 1
    )
    decay_mat = jnp.where(causal, jnp.exp(jnp.where(causal, column - row, 0.0)), 0.0)
    lead = jnp.exp(column)
    tail = jnp.exp(total - column)
    held = state[...]
    held_half = held.astype(half)
    mixed = (dot_f32(query, key, (1, 1)) * decay_mat).astype(half)
    attn = dot_f32(mixed, value, (1, 0)) + lead * dot_f32(query, held_half, (1, 0))
    rms = jnp.sqrt(jnp.mean(attn * attn, axis=-1, keepdims=True) + eps_norm)
    normed = attn / rms
    upstream = upstream_ref[...].astype(jnp.float32)
    d_attn = (upstream - normed * jnp.mean(upstream * normed, axis=-1, keepdims=True)) / rms
    d_attn_b = d_attn.astype(half)
    carried_all[step] = dot_f32((query.astype(jnp.float32) * lead).astype(half), d_attn_b, (0, 0))
    d_mixed = (dot_f32(d_attn_b, value, (1, 1)) * decay_mat).astype(half)
    d_query = dot_f32(d_mixed, key, (1, 0)) + lead * dot_f32(d_attn_b, held_half, (1, 1))
    d_query_pre = d_query * (sig * (1.0 + query_pre * (1.0 - sig)))
    d_value = dot_f32(mixed, d_attn_b, (0, 0))
    gain = jnp.exp(total)
    state[...] = gain[:1, :] * held + dot_f32((key.astype(jnp.float32) * tail).astype(half), value, (0, 0))
    rows = pl.ds(pl.multiple_of(step * length, length), length)
    low_all[rows, :] = low
    key_all[rows, :] = key
    grads[rows, :size] = d_query_pre
    grads[rows, size:] = d_value

    @pl.when(step == steps - 1)
    def _():
        def back(i, later):
            block = steps - 1 - i
            at = pl.ds(pl.multiple_of(block * length, length), length)
            _, column, total = decays(block)
            tail = jnp.exp(total - column)
            grads[at, size:] += tail * dot_f32(key_all[at, :], later.astype(half), (1, 0))
            return carried_all[block] + jnp.exp(total)[:1, :] * later

        lax.fori_loop(0, steps, back, jnp.zeros(state.shape, jnp.float32))
        both = grads[...].astype(half)
        low_grad_ref[...] = dot_f32(both, lift_ref[...], (1, 1))
        ups = dot_f32(low_all[...], both, (0, 0))
        up_ref[0] = adapter_scale * ups[:rank, :size]
        up_ref[1] = adapter_scale * ups[rank:, size:]


def head_on_device(
    tokens,
    query_weight,
    key_weight,
    value_weight,
    adapter_down_maps,
    lifting_matrices,
    decay_logarithms,
    output_gradient,
):
    seq_count = lax.axis_size("seq")
    model_count = lax.axis_size("mp")
    length, width = tokens.shape
    heads = decay_logarithms.shape[0]
    size = query_weight.shape[1] // heads
    rank = lifting_matrices.shape[1]
    tokens_all = lax.all_gather(tokens, "seq", axis=0, tiled=True)
    weights = jnp.stack([query_weight, key_weight, value_weight])
    weights = lax.all_to_all(weights, "seq", split_axis=2, concat_axis=1, tiled=True)
    upstream = lax.all_to_all(output_gradient, "seq", split_axis=1, concat_axis=0, tiled=True)
    cumulative = jnp.cumsum(decay_logarithms, axis=1)
    cumulative = lax.all_to_all(cumulative, "seq", split_axis=0, concat_axis=1, tiled=True)
    cumulative = cumulative.reshape(seq_count, length)
    weight = jnp.concatenate([weights[0], weights[1], weights[2], adapter_down_maps], axis=1)
    lift = lax.dynamic_slice_in_dim(lifting_matrices, lax.axis_index("seq") * size, size, 2)
    lift = (adapter_scale * lift).astype(jnp.bfloat16)
    empty = jnp.zeros_like(lift[0])
    lift = jnp.concatenate(
        [jnp.concatenate([lift[0], empty], axis=1), jnp.concatenate([empty, lift[1]], axis=1)], axis=0
    )
    total_tokens = length * seq_count
    low_gradient, up_products = pl.pallas_call(
        functools.partial(layer_kernel, rank),
        grid=(seq_count,),
        out_shape=(
            jax.ShapeDtypeStruct((total_tokens, 2 * rank), jnp.float32),
            jax.ShapeDtypeStruct((2, rank, size), jnp.float32),
        ),
        in_specs=[
            pl.BlockSpec((length, width), lambda i: (i, 0)),
            pl.BlockSpec(weight.shape, lambda i: (0, 0)),
            pl.BlockSpec(lift.shape, lambda i: (0, 0)),
            pl.BlockSpec(cumulative.shape, lambda i: (0, 0)),
            pl.BlockSpec((length, size), lambda i: (i, 0)),
        ],
        out_specs=(
            pl.BlockSpec((total_tokens, 2 * rank), lambda i: (0, 0)),
            pl.BlockSpec((2, rank, size), lambda i: (0, 0, 0)),
        ),
        scratch_shapes=[
            pltpu.VMEM((size, size), jnp.float32),
            pltpu.VMEM((total_tokens, 2 * rank), jnp.bfloat16),
            pltpu.VMEM((total_tokens, size), jnp.bfloat16),
            pltpu.VMEM((seq_count, size, size), jnp.float32),
            pltpu.VMEM((total_tokens, 2 * size), jnp.float32),
        ],
        compiler_params=pltpu.CompilerParams(
            dimension_semantics=("arbitrary",), vmem_limit_bytes=48 * 1024 * 1024
        ),
    )(tokens_all, weight, lift, cumulative, upstream)
    grad_up = lax.all_gather(up_products, "seq", axis=2, tiled=True)
    whole_low = lax.psum(low_gradient, ("seq", "mp"))
    own_rows = width // (seq_count * model_count)
    place = lax.axis_index("seq") * model_count + lax.axis_index("mp")
    mine = lax.dynamic_slice_in_dim(tokens_all, place * own_rows, own_rows, 1)
    grad_down = lax.dot_general(
        mine, whole_low.astype(jnp.bfloat16), (((0,), (0,)), ((), ())), preferred_element_type=jnp.float32
    )
    return (grad_down, grad_up)


def per_device(*arrays):
    decay = arrays[6]
    one_head = decay.shape[0] == lax.axis_size("seq")
    square = decay.shape[1] == arrays[1].shape[1] // decay.shape[0]
    return (head_on_device if one_head and square else on_device)(*arrays)


def solution(mesh):
    return jax.shard_map(
        per_device,
        mesh=mesh,
        in_specs=(
            P("seq", None),
            P("seq", "mp"),
            P("seq", "mp"),
            P("seq", "mp"),
            P(),
            P(None, None, "mp"),
            P("mp", "seq"),
            P("seq", "mp"),
        ),
        out_specs=(P(("seq", "mp"), None), P(None, None, "mp")),
        check_vma=False,
    )
```

```python
import functools

import jax
import jax.numpy as jnp
from jax import lax
from jax.experimental import pallas as pl
from jax.experimental.pallas import tpu as pltpu
from jax.sharding import PartitionSpec as P

adapter_scale = 2.0
eps_norm = 1e-06
exact_arithmetic = lax.Precision.HIGHEST


def carried_in(value, axis, join, neutral, backward):
    count, mine = (lax.axis_size(axis), lax.axis_index(axis))
    pieces = jax.tree.map(lambda part: lax.all_gather(part, axis), value)
    if backward:
        pieces = jax.tree.map(lambda part: part[::-1], pieces)
        mine = count - 1 - mine
    so_far = jax.tree.map(
        lambda part, zero: jnp.full_like(part, 0) + jnp.asarray(zero, part.dtype), value, neutral
    )

    def hop(position, so_far):
        longer = join(so_far, jax.tree.map(lambda part: part[position], pieces))
        return jax.tree.map(lambda new, old: jnp.where(position < mine, new, old), longer, so_far)

    return lax.fori_loop(0, count - 1, hop, so_far)


def combine(earlier, later):
    return (earlier[0] * later[0], later[0][:, None, None] * earlier[1] + later[1])


def split_heads(flat, heads):
    return flat.reshape(flat.shape[0], heads, flat.shape[1] // heads).transpose(1, 0, 2)


def join_heads(arr):
    return arr.transpose(1, 0, 2).reshape(arr.shape[1], arr.shape[0] * arr.shape[2])


def on_device(
    tokens,
    query_weight,
    key_weight,
    value_weight,
    adapter_down_maps,
    lifting_matrices,
    decay_logarithms,
    output_gradient,
):
    length = tokens.shape[0]
    heads = decay_logarithms.shape[0]
    rank_index = lifting_matrices.shape[1]
    low_product = jnp.dot(tokens, adapter_down_maps, preferred_element_type=jnp.float32).astype(
        jnp.bfloat16
    )
    query_low_product = low_product[:, :rank_index]
    value_low_product = low_product[:, rank_index:]
    cumulative = jnp.cumsum(decay_logarithms, axis=1)
    total = cumulative[:, -1]
    gain = jnp.exp(total)
    tail = jnp.exp(total[:, None] - cumulative)
    lead = jnp.exp(cumulative)
    causal = jnp.arange(length)[:, None] >= jnp.arange(length)[None, :]
    spread = cumulative[:, :, None] - cumulative[:, None, :]
    decay_mat = jnp.where(causal[None], jnp.exp(jnp.where(causal[None], spread, 0.0)), 0.0)
    pieces = (
        lax.all_gather(query_weight, "seq", axis=0, tiled=True),
        lax.all_gather(key_weight, "seq", axis=0, tiled=True),
        lax.all_gather(value_weight, "seq", axis=0, tiled=True),
    )
    columns = tokens
    query_frozen_part, key_base, value_frozen_part = tuple(
        (jnp.dot(columns, piece, preferred_element_type=jnp.float32) for piece in pieces)
    )
    value_before_norm = value_frozen_part + adapter_scale * jnp.dot(
        value_low_product, lifting_matrices[1], preferred_element_type=jnp.float32
    )
    key_heads = split_heads(jax.nn.silu(key_base).astype(jnp.bfloat16), heads)
    value_heads = split_heads(value_before_norm.astype(jnp.bfloat16), heads)
    key_f = key_heads.astype(jnp.float32)
    local = jnp.einsum(
        "hsi,hsj->hij",
        key_f * tail[:, :, None],
        value_heads.astype(jnp.float32),
        precision=exact_arithmetic,
    )
    state_in = carried_in(
        (gain, local), "seq", combine, (jnp.ones_like(gain), jnp.zeros_like(local)), False
    )[1]
    key_heads, key_f, value_heads, state_in = (key_heads, key_f, value_heads, state_in)
    query_before_norm = query_frozen_part + adapter_scale * jnp.dot(
        query_low_product, lifting_matrices[0], preferred_element_type=jnp.float32
    )
    query_heads = split_heads(jax.nn.silu(query_before_norm).astype(jnp.bfloat16), heads)
    query_f = query_heads.astype(jnp.float32)
    scores = jnp.einsum("htd,hsd->hts", query_heads, key_heads, preferred_element_type=jnp.float32)
    mixed = (scores * decay_mat).astype(jnp.bfloat16)
    attn = jnp.einsum(
        "hts,hsj->htj", mixed, value_heads, preferred_element_type=jnp.float32
    ) + lead[:, :, None] * jnp.einsum("hti,hij->htj", query_f, state_in, precision=exact_arithmetic)
    rms = jnp.sqrt(jnp.mean(attn * attn, axis=-1, keepdims=True) + eps_norm)
    normed = attn / rms
    upstream = split_heads(output_gradient, heads).astype(jnp.float32)
    d_attn = (upstream - normed * jnp.mean(upstream * normed, axis=-1, keepdims=True)) / rms
    d_attn_b = d_attn.astype(jnp.bfloat16)
    carried = jnp.einsum(
        "hti,htj->hij", query_f * lead[:, :, None], d_attn, precision=exact_arithmetic
    )
    later = carried_in(
        (gain, carried), "seq", combine, (jnp.ones_like(gain), jnp.zeros_like(carried)), True
    )[1]
    d_mixed = (
        jnp.einsum("htj,hsj->hts", d_attn_b, value_heads, preferred_element_type=jnp.float32)
        * decay_mat
    ).astype(jnp.bfloat16)
    d_query = jnp.einsum(
        "hts,hsi->hti", d_mixed, key_heads, preferred_element_type=jnp.float32
    ) + lead[:, :, None] * jnp.einsum("htj,hij->hti", d_attn, state_in, precision=exact_arithmetic)
    d_value = jnp.einsum(
        "hts,htj->hsj", mixed, d_attn_b, preferred_element_type=jnp.float32
    ) + tail[:, :, None] * jnp.einsum("hsi,hij->hsj", key_f, later, precision=exact_arithmetic)
    sig = jax.nn.sigmoid(query_before_norm)
    query_pre_gradient = join_heads(d_query) * (sig * (1.0 + query_before_norm * (1.0 - sig)))
    value_flat_gradient = join_heads(d_value)
    low_product_float = low_product.astype(jnp.float32)
    up_products = jnp.stack(
        [
            adapter_scale
            * jnp.dot(
                low_product_float[:, :rank_index].T, query_pre_gradient, precision=exact_arithmetic
            ),
            adapter_scale
            * jnp.dot(
                low_product_float[:, rank_index:].T, value_flat_gradient, precision=exact_arithmetic
            ),
        ]
    )
    grad_up = lax.psum(up_products, "seq")
    low_gradient = adapter_scale * jnp.concatenate(
        [
            jnp.dot(
                query_pre_gradient,
                lifting_matrices[0].astype(jnp.float32).T,
                precision=exact_arithmetic,
            ),
            jnp.dot(
                value_flat_gradient,
                lifting_matrices[1].astype(jnp.float32).T,
                precision=exact_arithmetic,
            ),
        ],
        axis=1,
    )
    seq_count = lax.axis_size("seq")
    model_count = lax.axis_size("mp")
    own_rows = tokens.shape[1] // (seq_count * model_count)
    whole_low = lax.psum(low_gradient, "mp")
    grouped = tokens.reshape(length, seq_count, model_count, own_rows)
    mine = lax.dynamic_index_in_dim(grouped, lax.axis_index("mp"), 2, keepdims=False).reshape(
        length, seq_count * own_rows
    )
    columns = mine.astype(jnp.float32)
    grad_down = lax.psum_scatter(
        jnp.dot(columns.T, whole_low, precision=exact_arithmetic),
        "seq",
        scatter_dimension=0,
        tiled=True,
    )
    return (grad_down, grad_up)


def dot_f32(a, b, contract):
    return lax.dot_general(a, b, ((contract[:1], contract[1:]), ((), ())), preferred_element_type=jnp.float32)


def layer_kernel(
    rank,
    tokens_ref,
    weight_ref,
    lift_ref,
    cumulative_ref,
    upstream_ref,
    low_grad_ref,
    up_ref,
    state,
    low_all,
    key_all,
    carried_all,
    grads,
):
    step = pl.program_id(0)
    steps = pl.num_programs(0)
    length = tokens_ref.shape[0]
    size = state.shape[0]
    half = jnp.bfloat16

    def decays(block):
        at = block * steps + lax.axis_index("seq")
        row = jnp.broadcast_to(cumulative_ref[pl.ds(at, 1), :], (length, length))
        column = row.T
        last = row[:, length - 1 :]
        return row, column, jnp.broadcast_to(last, (length, length))

    @pl.when(step == 0)
    def _():
        state[...] = jnp.zeros_like(state)

    product = jnp.dot(tokens_ref[...], weight_ref[...], preferred_element_type=jnp.float32)
    low = product[:, 3 * size :].astype(half)
    lifted = jnp.dot(low, lift_ref[...], preferred_element_type=jnp.float32)
    query_pre = product[:, :size] + lifted[:, :size]
    key_pre = product[:, size : 2 * size]
    value = (product[:, 2 * size : 3 * size] + lifted[:, size:]).astype(half)
    sig = jax.nn.sigmoid(query_pre)
    query = (query_pre * sig).astype(half)
    key = (key_pre * jax.nn.sigmoid(key_pre)).astype(half)
    row, column, total = decays(step)
    causal = lax.broadcasted_iota(jnp.int32, (length, length), 0) >= lax.broadcasted_iota(
        jnp.int32, (length, length), 1
    )
    decay_mat = jnp.where(causal, jnp.exp(jnp.where(causal, column - row, 0.0)), 0.0)
    lead = jnp.exp(column)
    tail = jnp.exp(total - column)
    held = state[...]
    held_half = held.astype(half)
    mixed = (dot_f32(query, key, (1, 1)) * decay_mat).astype(half)
    attn = dot_f32(mixed, value, (1, 0)) + lead * dot_f32(query, held_half, (1, 0))
    rms = jnp.sqrt(jnp.mean(attn * attn, axis=-1, keepdims=True) + eps_norm)
    normed = attn / rms
    upstream = upstream_ref[...].astype(jnp.float32)
    d_attn = (upstream - normed * jnp.mean(upstream * normed, axis=-1, keepdims=True)) / rms
    d_attn_b = d_attn.astype(half)
    carried_all[step] = dot_f32((query.astype(jnp.float32) * lead).astype(half), d_attn_b, (0, 0))
    d_mixed = (dot_f32(d_attn_b, value, (1, 1)) * decay_mat).astype(half)
    d_query = dot_f32(d_mixed, key, (1, 0)) + lead * dot_f32(d_attn_b, held_half, (1, 1))
    d_query_pre = d_query * (sig * (1.0 + query_pre * (1.0 - sig)))
    d_value = dot_f32(mixed, d_attn_b, (0, 0))
    gain = jnp.exp(total)
    state[...] = gain[:1, :] * held + dot_f32((key.astype(jnp.float32) * tail).astype(half), value, (0, 0))
    rows = pl.ds(pl.multiple_of(step * length, length), length)
    low_all[rows, :] = low
    key_all[rows, :] = key
    grads[rows, :size] = d_query_pre
    grads[rows, size:] = d_value

    @pl.when(step == steps - 1)
    def _():
        def back(i, later):
            block = steps - 1 - i
            at = pl.ds(pl.multiple_of(block * length, length), length)
            _, column, total = decays(block)
            tail = jnp.exp(total - column)
            grads[at, size:] += tail * dot_f32(key_all[at, :], later.astype(half), (1, 0))
            return carried_all[block] + jnp.exp(total)[:1, :] * later

        lax.fori_loop(0, steps, back, jnp.zeros(state.shape, jnp.float32))
        both = grads[...].astype(half)
        low_grad_ref[...] = dot_f32(both, lift_ref[...], (1, 1)).astype(half)
        ups = dot_f32(low_all[...], both, (0, 0))
        up_ref[0] = adapter_scale * ups[:rank, :size]
        up_ref[1] = adapter_scale * ups[rank:, size:]


MESH = pl.DeviceIdType.MESH


def exchange_kernel(
    tokens_ref,
    query_ref,
    key_ref,
    value_ref,
    down_ref,
    upstream_ref,
    cumulative_ref,
    tokens_all,
    weight_all,
    upstream_all,
    cumulative_all,
    local_sem,
    token_send,
    token_recv,
    block_send,
    block_recv,
):
    count = lax.axis_size("seq")
    me, x = lax.axis_index("seq"), lax.axis_index("mp")
    core, y, z = lax.rem(me, 2), lax.rem(me // 2, 2), me // 4
    layers = count // 4
    length = tokens_ref.shape[0]
    half = length // 2
    depth = query_ref.shape[0]
    size = upstream_all.shape[1]
    heads = cumulative_ref.shape[0]
    barrier = pltpu.get_barrier_semaphore()

    def greet(j, carry):
        pl.semaphore_signal(
            barrier, inc=1, device_id=(lax.rem(me + j, count), x), device_id_type=MESH
        )
        return carry

    lax.fori_loop(1, count, greet, 0)
    pl.semaphore_signal(barrier, inc=1, device_id=(me, 1 - x), device_id_type=MESH)
    pl.semaphore_wait(barrier, count)

    def seq_of(zz, yy, cc):
        return (zz * 2 + yy) * 2 + cc

    def rows_of(block, part):
        return pl.ds(pl.multiple_of(block * length + part * half, half), half)

    sent = []

    def send(block, part, device, own=False):
        source = (
            tokens_ref.at[pl.ds(pl.multiple_of(part * half, half), half), :]
            if own
            else tokens_all.at[rows_of(block, part), :]
        )
        copy = pltpu.make_async_remote_copy(
            src_ref=source,
            dst_ref=tokens_all.at[rows_of(block, part), :],
            send_sem=token_send.at[len(sent)],
            recv_sem=token_recv.at[block * 2 + part],
            device_id=device,
            device_id_type=MESH,
        )
        copy.start()
        sent.append(copy)

    def arrived(block, part):
        at = tokens_all.at[rows_of(block, part), :]
        pltpu.make_async_copy(at, at, token_recv.at[block * 2 + part]).wait()

    over_y = (seq_of(z, 1 - y, core), x)
    over_x = (me, 1 - x)
    sibling = (seq_of(z, y, 1 - core), x)
    weights = (query_ref, key_ref, value_ref)

    def block_copies(j, source, target):
        to = (target, x)
        pairs = [
            (
                weight.at[:, pl.ds(pl.multiple_of(target * size, size), size)],
                weight_all.at[
                    pl.ds(pl.multiple_of(source * depth, depth), depth), k * size : (k + 1) * size
                ],
            )
            for k, weight in enumerate(weights)
        ]
        pairs.append(
            (
                upstream_ref.at[:, pl.ds(pl.multiple_of(target * size, size), size)],
                upstream_all.at[pl.ds(pl.multiple_of(source * length, length), length), :],
            )
        )
        pairs.append(
            (
                cumulative_ref,
                cumulative_all.at[pl.ds(pl.multiple_of(source * heads, heads), heads), :],
            )
        )
        return [
            pltpu.make_async_remote_copy(
                src_ref=source_ref,
                dst_ref=dst_ref,
                send_sem=block_send.at[k, j],
                recv_sem=block_recv.at[k, j],
                device_id=to,
                device_id_type=MESH,
            )
            for k, (source_ref, dst_ref) in enumerate(pairs)
        ], pairs

    for j in range(1, layers):
        send(me, x, (seq_of(lax.rem(z + j, layers), y, core), x), own=True)
    send(me, x, over_y, own=True)
    send(me, 0, sibling, own=True)
    send(me, 1, sibling, own=True)

    def start_blocks(j, carry):
        for copy in block_copies(j, me, lax.rem(me + j, count))[0]:
            copy.start()
        return carry

    lax.fori_loop(1, count, start_blocks, 0)
    mine = [(tokens_ref, tokens_all.at[pl.ds(pl.multiple_of(me * length, length), length), :])]
    mine += block_copies(0, me, me)[1]
    mine.append((down_ref, weight_all.at[:, 3 * size :]))
    local = [
        pltpu.make_async_copy(a, b, local_sem.at[k]) for k, (a, b) in enumerate(mine)
    ]
    for copy in local:
        copy.start()

    def along_z(j):
        block = seq_of(lax.rem(z - j + layers, layers), y, core)
        arrived(block, x)
        send(block, x, over_y)
        send(block, x, over_x)
        send(block, x, sibling)

    def along_y(j):
        block = seq_of(lax.rem(z - j + layers, layers), 1 - y, core)
        arrived(block, x)
        send(block, x, over_x)
        send(block, x, sibling)

    def along_x(j):
        for other in range(2) if j else (1,):
            yy = 1 - y if other else y
            block = seq_of(lax.rem(z - j + layers, layers), yy, core)
            arrived(block, 1 - x)
            send(block, 1 - x, sibling)

    for step in range(layers + 2):
        if 1 <= step + 1 < layers:
            along_z(step + 1)
        if step < layers:
            along_y(step)
        if 0 <= step - 1 < layers:
            along_x(step - 1)
    for zz in range(layers):
        for yy in range(2):
            for part in range(2):
                arrived(seq_of(zz, yy, 1 - core), part)

    def end_blocks(j, carry):
        source = lax.rem(me - j + count, count)
        for copy in block_copies(j, source, me)[0]:
            copy.wait_recv()
        for copy in block_copies(j, me, lax.rem(me + j, count))[0]:
            copy.wait_send()
        return carry

    lax.fori_loop(1, count, end_blocks, 0)
    for copy in local:
        copy.wait()
    for copy in sent:
        copy.wait_send()


def reduce_kernel(
    low_ref,
    up_ref,
    tokens_all,
    down_out,
    up_out,
    pieces,
    whole,
    window,
    product,
    window_sem,
    piece_send,
    piece_recv,
    whole_send,
    whole_recv,
    up_send,
    up_recv,
):
    seq_count, model_count = lax.axis_size("seq"), lax.axis_size("mp")
    count = seq_count * model_count
    seq, x = lax.axis_index("seq"), lax.axis_index("mp")
    me = seq * model_count + x
    rows = low_ref.shape[0] // count
    size = up_ref.shape[2]
    width = tokens_all.shape[1]
    own = down_out.shape[0]
    span = window.shape[1]
    barrier = pltpu.get_barrier_semaphore()
    first = jnp.minimum(me * own // 128, (width - span) // 128)
    load = pltpu.make_async_copy(
        tokens_all.at[:, pl.ds(pl.multiple_of(first * 128, 128), span)], window, window_sem
    )
    load.start()

    def device(j):
        to = lax.rem(me + j, count)
        return to, (to // model_count, lax.rem(to, model_count))

    def greet(j, carry):
        pl.semaphore_signal(barrier, inc=1, device_id=device(j)[1], device_id_type=MESH)
        return carry

    lax.fori_loop(1, count, greet, 0)
    pl.semaphore_wait(barrier, count - 1)

    def at(block):
        return pl.ds(pl.multiple_of(block * rows, rows), rows)

    def piece_copy(j):
        to, where = device(j)
        return pltpu.make_async_remote_copy(
            src_ref=low_ref.at[at(to), :],
            dst_ref=pieces.at[j],
            send_sem=piece_send.at[j],
            recv_sem=piece_recv.at[j],
            device_id=where,
            device_id_type=MESH,
        )

    def whole_copy(j, block):
        return pltpu.make_async_remote_copy(
            src_ref=whole.at[at(block), :],
            dst_ref=whole.at[at(block), :],
            send_sem=whole_send.at[j],
            recv_sem=whole_recv.at[j],
            device_id=device(j)[1],
            device_id_type=MESH,
        )

    def up_copy(j, block):
        return pltpu.make_async_remote_copy(
            src_ref=up_ref,
            dst_ref=up_out.at[:, :, pl.ds(pl.multiple_of(block * size, size), size)],
            send_sem=up_send.at[j],
            recv_sem=up_recv.at[j],
            device_id=(lax.rem(seq + j, seq_count), x),
            device_id_type=MESH,
        )

    def loop(start, stop, act):
        def body(j, carry):
            act(j)
            return carry

        lax.fori_loop(start, stop, body, 0)

    loop(1, count, lambda j: piece_copy(j).start())
    loop(1, seq_count, lambda j: up_copy(j, seq).start())
    up_out[:, :, pl.ds(pl.multiple_of(seq * size, size), size)] = up_ref[...]

    def add(j, total):
        piece_copy(j).wait_recv()
        return total + pieces[j].astype(jnp.float32)

    total = lax.fori_loop(1, count, add, low_ref[at(me), :].astype(jnp.float32))
    whole[at(me), :] = total.astype(jnp.bfloat16)
    loop(1, count, lambda j: whole_copy(j, me).start())
    loop(1, count, lambda j: whole_copy(j, lax.rem(me - j + count, count)).wait_recv())
    load.wait()
    product[...] = dot_f32(window[...], whole[...], (0, 0))
    down_out[...] = product[pl.ds(pl.multiple_of(me * own - first * 128, 8), own), :]
    loop(1, count, lambda j: piece_copy(j).wait_send())
    loop(1, count, lambda j: whole_copy(j, me).wait_send())
    loop(1, seq_count, lambda j: up_copy(j, lax.rem(seq - j + seq_count, seq_count)).wait_recv())
    loop(1, seq_count, lambda j: up_copy(j, seq).wait_send())


def head_on_device(
    tokens,
    query_weight,
    key_weight,
    value_weight,
    adapter_down_maps,
    lifting_matrices,
    decay_logarithms,
    output_gradient,
):
    seq_count = lax.axis_size("seq")
    model_count = lax.axis_size("mp")
    length, width = tokens.shape
    heads = decay_logarithms.shape[0]
    size = query_weight.shape[1] // heads
    rank = lifting_matrices.shape[1]
    cumulative = jnp.cumsum(decay_logarithms, axis=1)
    half = jnp.bfloat16
    total_tokens = length * seq_count
    anywhere = pl.BlockSpec(memory_space=pl.ANY)
    in_vmem = pl.BlockSpec(memory_space=pltpu.VMEM)
    dma = pltpu.SemaphoreType.DMA
    layers = seq_count // 4
    token_copies = (layers - 1) * 4 + 3 + layers * 2 + 2 * layers - 1
    tokens_all, weight, upstream, cumulative = pl.pallas_call(
        exchange_kernel,
        out_shape=(
            jax.ShapeDtypeStruct((total_tokens, width), half),
            jax.ShapeDtypeStruct((width, 3 * size + 2 * rank), half),
            jax.ShapeDtypeStruct((total_tokens, size), half),
            jax.ShapeDtypeStruct((seq_count * heads, length), jnp.float32),
        ),
        in_specs=[anywhere] * 7,
        out_specs=(anywhere,) * 4,
        scratch_shapes=[
            dma((7,)),
            dma((token_copies,)),
            dma((2 * seq_count,)),
            dma((5, seq_count)),
            dma((5, seq_count)),
        ],
        compiler_params=pltpu.CompilerParams(collective_id=0, has_side_effects=True),
    )(
        tokens,
        query_weight,
        key_weight,
        value_weight,
        adapter_down_maps,
        output_gradient,
        cumulative,
    )
    lift = lax.dynamic_slice_in_dim(lifting_matrices, lax.axis_index("seq") * size, size, 2)
    lift = (adapter_scale * lift).astype(jnp.bfloat16)
    empty = jnp.zeros_like(lift[0])
    lift = jnp.concatenate(
        [jnp.concatenate([lift[0], empty], axis=1), jnp.concatenate([empty, lift[1]], axis=1)], axis=0
    )
    low_gradient, up_products = pl.pallas_call(
        functools.partial(layer_kernel, rank),
        grid=(seq_count,),
        out_shape=(
            jax.ShapeDtypeStruct((total_tokens, 2 * rank), half),
            jax.ShapeDtypeStruct((2, rank, size), jnp.float32),
        ),
        in_specs=[
            pl.BlockSpec((length, width), lambda i: (i, 0)),
            pl.BlockSpec(weight.shape, lambda i: (0, 0)),
            pl.BlockSpec(lift.shape, lambda i: (0, 0)),
            pl.BlockSpec(cumulative.shape, lambda i: (0, 0)),
            pl.BlockSpec((length, size), lambda i: (i, 0)),
        ],
        out_specs=(
            pl.BlockSpec((total_tokens, 2 * rank), lambda i: (0, 0)),
            pl.BlockSpec((2, rank, size), lambda i: (0, 0, 0)),
        ),
        scratch_shapes=[
            pltpu.VMEM((size, size), jnp.float32),
            pltpu.VMEM((total_tokens, 2 * rank), jnp.bfloat16),
            pltpu.VMEM((total_tokens, size), jnp.bfloat16),
            pltpu.VMEM((seq_count, size, size), jnp.float32),
            pltpu.VMEM((total_tokens, 2 * size), jnp.float32),
        ],
        compiler_params=pltpu.CompilerParams(
            dimension_semantics=("arbitrary",), vmem_limit_bytes=48 * 1024 * 1024
        ),
    )(tokens_all, weight, lift, cumulative, upstream)
    count = seq_count * model_count
    own_rows = width // count
    span = 256
    grad_down, grad_up = pl.pallas_call(
        reduce_kernel,
        out_shape=(
            jax.ShapeDtypeStruct((own_rows, 2 * rank), jnp.float32),
            jax.ShapeDtypeStruct((2, rank, size * seq_count), jnp.float32),
        ),
        in_specs=[in_vmem, in_vmem, anywhere],
        out_specs=(in_vmem, in_vmem),
        scratch_shapes=[
            pltpu.VMEM((count, total_tokens // count, 2 * rank), half),
            pltpu.VMEM((total_tokens, 2 * rank), half),
            pltpu.VMEM((total_tokens, span), half),
            pltpu.VMEM((span, 2 * rank), jnp.float32),
            dma(()),
            dma((count,)),
            dma((count,)),
            dma((count,)),
            dma((count,)),
            dma((seq_count,)),
            dma((seq_count,)),
        ],
        compiler_params=pltpu.CompilerParams(
            collective_id=1, has_side_effects=True, vmem_limit_bytes=32 * 1024 * 1024
        ),
    )(low_gradient, up_products, tokens_all)
    return (grad_down, grad_up)


def per_device(*arrays):
    length, width = arrays[0].shape
    heads = arrays[6].shape[0]
    seq_count, model_count = lax.axis_size("seq"), lax.axis_size("mp")
    size = arrays[1].shape[1] // heads
    rank = arrays[5].shape[1]
    own_rows = width // (seq_count * model_count)
    fits = (
        heads == seq_count
        and seq_count % 4 == 0
        and model_count == 2
        and length == size == 2 * rank == 128
        and arrays[1].shape[0] % 16 == 0
        and heads % 8 == 0
        and own_rows % 8 == 0
        and own_rows <= 128
        and (length // model_count) % 16 == 0
    )
    return (head_on_device if fits else on_device)(*arrays)


def solution(mesh):
    return jax.shard_map(
        per_device,
        mesh=mesh,
        in_specs=(
            P("seq", None),
            P("seq", "mp"),
            P("seq", "mp"),
            P("seq", "mp"),
            P(),
            P(None, None, "mp"),
            P("mp", "seq"),
            P("seq", "mp"),
        ),
        out_specs=(P(("seq", "mp"), None), P(None, None, "mp")),
        check_vma=False,
    )
```

```python
import functools

import jax
import jax.numpy as jnp
from jax import lax
from jax.experimental import pallas as pl
from jax.experimental.pallas import tpu as pltpu
from jax.sharding import PartitionSpec as P

adapter_scale = 2.0
eps_norm = 1e-06
exact_arithmetic = lax.Precision.HIGHEST


def carried_in(value, axis, join, neutral, backward):
    count, mine = (lax.axis_size(axis), lax.axis_index(axis))
    pieces = jax.tree.map(lambda part: lax.all_gather(part, axis), value)
    if backward:
        pieces = jax.tree.map(lambda part: part[::-1], pieces)
        mine = count - 1 - mine
    so_far = jax.tree.map(
        lambda part, zero: jnp.full_like(part, 0) + jnp.asarray(zero, part.dtype), value, neutral
    )

    def hop(position, so_far):
        longer = join(so_far, jax.tree.map(lambda part: part[position], pieces))
        return jax.tree.map(lambda new, old: jnp.where(position < mine, new, old), longer, so_far)

    return lax.fori_loop(0, count - 1, hop, so_far)


def combine(earlier, later):
    return (earlier[0] * later[0], later[0][:, None, None] * earlier[1] + later[1])


def split_heads(flat, heads):
    return flat.reshape(flat.shape[0], heads, flat.shape[1] // heads).transpose(1, 0, 2)


def join_heads(arr):
    return arr.transpose(1, 0, 2).reshape(arr.shape[1], arr.shape[0] * arr.shape[2])


def on_device(
    tokens,
    query_weight,
    key_weight,
    value_weight,
    adapter_down_maps,
    lifting_matrices,
    decay_logarithms,
    output_gradient,
):
    length = tokens.shape[0]
    heads = decay_logarithms.shape[0]
    rank_index = lifting_matrices.shape[1]
    low_product = jnp.dot(tokens, adapter_down_maps, preferred_element_type=jnp.float32).astype(
        jnp.bfloat16
    )
    query_low_product = low_product[:, :rank_index]
    value_low_product = low_product[:, rank_index:]
    cumulative = jnp.cumsum(decay_logarithms, axis=1)
    total = cumulative[:, -1]
    gain = jnp.exp(total)
    tail = jnp.exp(total[:, None] - cumulative)
    lead = jnp.exp(cumulative)
    causal = jnp.arange(length)[:, None] >= jnp.arange(length)[None, :]
    spread = cumulative[:, :, None] - cumulative[:, None, :]
    decay_mat = jnp.where(causal[None], jnp.exp(jnp.where(causal[None], spread, 0.0)), 0.0)
    pieces = (
        lax.all_gather(query_weight, "seq", axis=0, tiled=True),
        lax.all_gather(key_weight, "seq", axis=0, tiled=True),
        lax.all_gather(value_weight, "seq", axis=0, tiled=True),
    )
    columns = tokens
    query_frozen_part, key_base, value_frozen_part = tuple(
        (jnp.dot(columns, piece, preferred_element_type=jnp.float32) for piece in pieces)
    )
    value_before_norm = value_frozen_part + adapter_scale * jnp.dot(
        value_low_product, lifting_matrices[1], preferred_element_type=jnp.float32
    )
    key_heads = split_heads(jax.nn.silu(key_base).astype(jnp.bfloat16), heads)
    value_heads = split_heads(value_before_norm.astype(jnp.bfloat16), heads)
    key_f = key_heads.astype(jnp.float32)
    local = jnp.einsum(
        "hsi,hsj->hij",
        key_f * tail[:, :, None],
        value_heads.astype(jnp.float32),
        precision=exact_arithmetic,
    )
    state_in = carried_in(
        (gain, local), "seq", combine, (jnp.ones_like(gain), jnp.zeros_like(local)), False
    )[1]
    key_heads, key_f, value_heads, state_in = (key_heads, key_f, value_heads, state_in)
    query_before_norm = query_frozen_part + adapter_scale * jnp.dot(
        query_low_product, lifting_matrices[0], preferred_element_type=jnp.float32
    )
    query_heads = split_heads(jax.nn.silu(query_before_norm).astype(jnp.bfloat16), heads)
    query_f = query_heads.astype(jnp.float32)
    scores = jnp.einsum("htd,hsd->hts", query_heads, key_heads, preferred_element_type=jnp.float32)
    mixed = (scores * decay_mat).astype(jnp.bfloat16)
    attn = jnp.einsum(
        "hts,hsj->htj", mixed, value_heads, preferred_element_type=jnp.float32
    ) + lead[:, :, None] * jnp.einsum("hti,hij->htj", query_f, state_in, precision=exact_arithmetic)
    rms = jnp.sqrt(jnp.mean(attn * attn, axis=-1, keepdims=True) + eps_norm)
    normed = attn / rms
    upstream = split_heads(output_gradient, heads).astype(jnp.float32)
    d_attn = (upstream - normed * jnp.mean(upstream * normed, axis=-1, keepdims=True)) / rms
    d_attn_b = d_attn.astype(jnp.bfloat16)
    carried = jnp.einsum(
        "hti,htj->hij", query_f * lead[:, :, None], d_attn, precision=exact_arithmetic
    )
    later = carried_in(
        (gain, carried), "seq", combine, (jnp.ones_like(gain), jnp.zeros_like(carried)), True
    )[1]
    d_mixed = (
        jnp.einsum("htj,hsj->hts", d_attn_b, value_heads, preferred_element_type=jnp.float32)
        * decay_mat
    ).astype(jnp.bfloat16)
    d_query = jnp.einsum(
        "hts,hsi->hti", d_mixed, key_heads, preferred_element_type=jnp.float32
    ) + lead[:, :, None] * jnp.einsum("htj,hij->hti", d_attn, state_in, precision=exact_arithmetic)
    d_value = jnp.einsum(
        "hts,htj->hsj", mixed, d_attn_b, preferred_element_type=jnp.float32
    ) + tail[:, :, None] * jnp.einsum("hsi,hij->hsj", key_f, later, precision=exact_arithmetic)
    sig = jax.nn.sigmoid(query_before_norm)
    query_pre_gradient = join_heads(d_query) * (sig * (1.0 + query_before_norm * (1.0 - sig)))
    value_flat_gradient = join_heads(d_value)
    low_product_float = low_product.astype(jnp.float32)
    up_products = jnp.stack(
        [
            adapter_scale
            * jnp.dot(
                low_product_float[:, :rank_index].T, query_pre_gradient, precision=exact_arithmetic
            ),
            adapter_scale
            * jnp.dot(
                low_product_float[:, rank_index:].T, value_flat_gradient, precision=exact_arithmetic
            ),
        ]
    )
    grad_up = lax.psum(up_products, "seq")
    low_gradient = adapter_scale * jnp.concatenate(
        [
            jnp.dot(
                query_pre_gradient,
                lifting_matrices[0].astype(jnp.float32).T,
                precision=exact_arithmetic,
            ),
            jnp.dot(
                value_flat_gradient,
                lifting_matrices[1].astype(jnp.float32).T,
                precision=exact_arithmetic,
            ),
        ],
        axis=1,
    )
    seq_count = lax.axis_size("seq")
    model_count = lax.axis_size("mp")
    own_rows = tokens.shape[1] // (seq_count * model_count)
    whole_low = lax.psum(low_gradient, "mp")
    grouped = tokens.reshape(length, seq_count, model_count, own_rows)
    mine = lax.dynamic_index_in_dim(grouped, lax.axis_index("mp"), 2, keepdims=False).reshape(
        length, seq_count * own_rows
    )
    columns = mine.astype(jnp.float32)
    grad_down = lax.psum_scatter(
        jnp.dot(columns.T, whole_low, precision=exact_arithmetic),
        "seq",
        scatter_dimension=0,
        tiled=True,
    )
    return (grad_down, grad_up)


def dot_f32(a, b, contract):
    return lax.dot_general(a, b, ((contract[:1], contract[1:]), ((), ())), preferred_element_type=jnp.float32)


def layer_kernel(
    rank,
    tokens_ref,
    weight_ref,
    lift_ref,
    cumulative_ref,
    upstream_ref,
    low_grad_ref,
    up_ref,
    state,
    low_all,
    key_all,
    carried_all,
    grads,
):
    step = pl.program_id(0)
    steps = pl.num_programs(0)
    length = tokens_ref.shape[0]
    size = state.shape[0]
    half = jnp.bfloat16

    def decays(block):
        at = block * steps + lax.axis_index("seq")
        row = jnp.broadcast_to(cumulative_ref[pl.ds(at, 1), :], (length, length))
        column = row.T
        last = row[:, length - 1 :]
        return row, column, jnp.broadcast_to(last, (length, length))

    @pl.when(step == 0)
    def _():
        state[...] = jnp.zeros_like(state)

    product = jnp.dot(tokens_ref[...], weight_ref[...], preferred_element_type=jnp.float32)
    low = product[:, 3 * size :].astype(half)
    lifted = jnp.dot(low, lift_ref[...], preferred_element_type=jnp.float32)
    query_pre = product[:, :size] + lifted[:, :size]
    key_pre = product[:, size : 2 * size]
    value = (product[:, 2 * size : 3 * size] + lifted[:, size:]).astype(half)
    sig = jax.nn.sigmoid(query_pre)
    query = (query_pre * sig).astype(half)
    key = (key_pre * jax.nn.sigmoid(key_pre)).astype(half)
    row, column, total = decays(step)
    causal = lax.broadcasted_iota(jnp.int32, (length, length), 0) >= lax.broadcasted_iota(
        jnp.int32, (length, length), 1
    )
    decay_mat = jnp.where(causal, jnp.exp(jnp.where(causal, column - row, 0.0)), 0.0)
    lead = jnp.exp(column)
    tail = jnp.exp(total - column)
    held = state[...]
    held_half = held.astype(half)
    mixed = (dot_f32(query, key, (1, 1)) * decay_mat).astype(half)
    attn = dot_f32(mixed, value, (1, 0)) + lead * dot_f32(query, held_half, (1, 0))
    rms = jnp.sqrt(jnp.mean(attn * attn, axis=-1, keepdims=True) + eps_norm)
    normed = attn / rms
    upstream = upstream_ref[...].astype(jnp.float32)
    d_attn = (upstream - normed * jnp.mean(upstream * normed, axis=-1, keepdims=True)) / rms
    d_attn_b = d_attn.astype(half)
    carried_all[step] = dot_f32((query.astype(jnp.float32) * lead).astype(half), d_attn_b, (0, 0))
    d_mixed = (dot_f32(d_attn_b, value, (1, 1)) * decay_mat).astype(half)
    d_query = dot_f32(d_mixed, key, (1, 0)) + lead * dot_f32(d_attn_b, held_half, (1, 1))
    d_query_pre = d_query * (sig * (1.0 + query_pre * (1.0 - sig)))
    d_value = dot_f32(mixed, d_attn_b, (0, 0))
    gain = jnp.exp(total)
    state[...] = gain[:1, :] * held + dot_f32((key.astype(jnp.float32) * tail).astype(half), value, (0, 0))
    rows = pl.ds(pl.multiple_of(step * length, length), length)
    low_all[rows, :] = low
    key_all[rows, :] = key
    grads[rows, :size] = d_query_pre
    grads[rows, size:] = d_value

    @pl.when(step == steps - 1)
    def _():
        def back(i, later):
            block = steps - 1 - i
            at = pl.ds(pl.multiple_of(block * length, length), length)
            _, column, total = decays(block)
            tail = jnp.exp(total - column)
            grads[at, size:] += tail * dot_f32(key_all[at, :], later.astype(half), (1, 0))
            return carried_all[block] + jnp.exp(total)[:1, :] * later

        lax.fori_loop(0, steps, back, jnp.zeros(state.shape, jnp.float32))
        both = grads[...].astype(half)
        low_grad_ref[...] = dot_f32(both, lift_ref[...], (1, 1)).astype(half)
        ups = dot_f32(low_all[...], both, (0, 0))
        up_ref[0] = adapter_scale * ups[:rank, :size]
        up_ref[1] = adapter_scale * ups[rank:, size:]


MESH = pl.DeviceIdType.MESH


def exchange_kernel(
    tokens_ref,
    query_ref,
    key_ref,
    value_ref,
    down_ref,
    upstream_ref,
    cumulative_ref,
    tokens_all,
    weight_all,
    upstream_all,
    cumulative_all,
    local_sem,
    hop_send,
    token_send,
    token_recv,
    block_send,
    block_recv,
):
    count = lax.axis_size("seq")
    me, x = lax.axis_index("seq"), lax.axis_index("mp")
    core, y, z = lax.rem(me, 2), lax.rem(me // 2, 2), me // 4
    layers = count // 4
    length = tokens_ref.shape[0]
    half = length // 2
    depth = query_ref.shape[0]
    size = upstream_all.shape[1]
    heads = cumulative_ref.shape[0]
    barrier = pltpu.get_barrier_semaphore()

    def greet(j, carry):
        pl.semaphore_signal(
            barrier, inc=1, device_id=(lax.rem(me + j, count), x), device_id_type=MESH
        )
        return carry

    lax.fori_loop(1, count, greet, 0)
    pl.semaphore_signal(barrier, inc=1, device_id=(me, 1 - x), device_id_type=MESH)
    pl.semaphore_wait(barrier, count)

    def seq_of(zz, yy, cc):
        return (zz * 2 + yy) * 2 + cc

    def rows_of(block, part):
        return pl.ds(pl.multiple_of(block * length + part * half, half), half)

    sent = []

    def send(block, part, device, own=False):
        source = (
            tokens_ref.at[pl.ds(pl.multiple_of(part * half, half), half), :]
            if own
            else tokens_all.at[rows_of(block, part), :]
        )
        copy = pltpu.make_async_remote_copy(
            src_ref=source,
            dst_ref=tokens_all.at[rows_of(block, part), :],
            send_sem=token_send.at[len(sent)],
            recv_sem=token_recv.at[block * 2 + part],
            device_id=device,
            device_id_type=MESH,
        )
        copy.start()
        sent.append(copy)

    def arrived(block, part):
        at = tokens_all.at[rows_of(block, part), :]
        pltpu.make_async_copy(at, at, token_recv.at[block * 2 + part]).wait()

    over_y = (seq_of(z, 1 - y, core), x)
    over_x = (me, 1 - x)
    sibling = (seq_of(z, y, 1 - core), x)
    weights = (query_ref, key_ref, value_ref)

    def block_copies(j, source, target):
        to = (target, x)
        pairs = [
            (
                weight.at[:, pl.ds(pl.multiple_of(target * size, size), size)],
                weight_all.at[
                    pl.ds(pl.multiple_of(source * depth, depth), depth), k * size : (k + 1) * size
                ],
            )
            for k, weight in enumerate(weights)
        ]
        pairs.append(
            (
                upstream_ref.at[:, pl.ds(pl.multiple_of(target * size, size), size)],
                upstream_all.at[pl.ds(pl.multiple_of(source * length, length), length), :],
            )
        )
        pairs.append(
            (
                cumulative_ref,
                cumulative_all.at[pl.ds(pl.multiple_of(source * heads, heads), heads), :],
            )
        )
        return [
            pltpu.make_async_remote_copy(
                src_ref=source_ref,
                dst_ref=dst_ref,
                send_sem=block_send.at[k, j],
                recv_sem=block_recv.at[k, j],
                device_id=to,
                device_id_type=MESH,
            )
            for k, (source_ref, dst_ref) in enumerate(pairs)
        ], pairs

    near = jnp.minimum(z, layers - 1 - z)

    def layer_at(j):
        side = jnp.where(2 * z < layers - 1, z + j - near, z - j + near)
        pair = z - (j + 1) // 2 if j % 2 else z + j // 2
        return z if j == 0 else jnp.where(j <= 2 * near, pair, side)

    hops = []

    def hop(block, up, own=False):
        to = jnp.where(up, z + 1, z - 1)
        inside = jnp.logical_and(to >= 0, to < layers)
        index = len(hops)

        def copy():
            part = pl.ds(pl.multiple_of(x * half, half), half)
            return pltpu.make_async_remote_copy(
                src_ref=tokens_ref.at[part, :] if own else tokens_all.at[rows_of(block, x), :],
                dst_ref=tokens_all.at[rows_of(block, x), :],
                send_sem=hop_send.at[index],
                recv_sem=token_recv.at[block * 2 + x],
                device_id=(seq_of(to, y, core), x),
                device_id_type=MESH,
            )

        hops.append((inside, copy))

        @pl.when(inside)
        def _():
            copy().start()

    hop(me, True, own=True)
    hop(me, False, own=True)
    send(me, x, over_y, own=True)
    send(me, 0, sibling, own=True)
    send(me, 1, sibling, own=True)

    def start_blocks(j, carry):
        for copy in block_copies(j, me, lax.rem(me + j, count))[0]:
            copy.start()
        return carry

    lax.fori_loop(1, count, start_blocks, 0)
    mine = [(tokens_ref, tokens_all.at[pl.ds(pl.multiple_of(me * length, length), length), :])]
    mine += block_copies(0, me, me)[1]
    mine.append((down_ref, weight_all.at[:, 3 * size :]))
    local = [
        pltpu.make_async_copy(a, b, local_sem.at[k]) for k, (a, b) in enumerate(mine)
    ]
    for copy in local:
        copy.start()

    def along_z(j):
        layer = layer_at(j)
        block = seq_of(layer, y, core)
        arrived(block, x)
        hop(block, layer < z)
        send(block, x, over_y)
        send(block, x, over_x)
        send(block, x, sibling)

    def along_y(j):
        block = seq_of(layer_at(j), 1 - y, core)
        arrived(block, x)
        send(block, x, over_x)
        send(block, x, sibling)

    def along_x(j):
        for other in range(2) if j else (1,):
            yy = 1 - y if other else y
            block = seq_of(layer_at(j), yy, core)
            arrived(block, 1 - x)
            send(block, 1 - x, sibling)

    for step in range(layers + 2):
        if 1 <= step + 1 < layers:
            along_z(step + 1)
        if step < layers:
            along_y(step)
        if 0 <= step - 1 < layers:
            along_x(step - 1)
    for zz in range(layers):
        for yy in range(2):
            for part in range(2):
                arrived(seq_of(zz, yy, 1 - core), part)

    def end_blocks(j, carry):
        source = lax.rem(me - j + count, count)
        for copy in block_copies(j, source, me)[0]:
            copy.wait_recv()
        for copy in block_copies(j, me, lax.rem(me + j, count))[0]:
            copy.wait_send()
        return carry

    lax.fori_loop(1, count, end_blocks, 0)
    for copy in local:
        copy.wait()
    for copy in sent:
        copy.wait_send()
    for inside, copy in hops:

        @pl.when(inside)
        def _(copy=copy):
            copy().wait_send()


def reduce_kernel(
    low_ref,
    up_ref,
    tokens_all,
    down_out,
    up_out,
    mate,
    summed,
    pieces,
    whole,
    window,
    product,
    window_sem,
    mate_sem,
    piece_send,
    piece_recv,
    whole_send,
    whole_recv,
    up_send,
    up_recv,
):
    chips = lax.axis_size("seq") // 2
    group = chips * 2
    seq, x = lax.axis_index("seq"), lax.axis_index("mp")
    chip, core = seq // 2, lax.rem(seq, 2)
    me, place = seq * 2 + x, chip * 2 + x
    rows = pieces.shape[1]
    size = up_ref.shape[2]
    width = tokens_all.shape[1]
    own = down_out.shape[0]
    span = window.shape[1]
    sibling = (chip * 2 + 1 - core, x)
    barrier = pltpu.get_barrier_semaphore()
    first = jnp.minimum(me * own // 128, (width - span) // 128)
    load = pltpu.make_async_copy(
        tokens_all.at[:, pl.ds(pl.multiple_of(first * 128, 128), span)], window, window_sem
    )
    load.start()

    def peer(j):
        to = lax.rem(place + j, group)
        return to // 2, lax.rem(to, 2)

    def device(j):
        to, to_x = peer(j)
        return to * 2 + core, to_x

    def loop(start, stop, act):
        def body(j, carry):
            act(j)
            return carry

        lax.fori_loop(start, stop, body, 0)

    def greet(where):
        pl.semaphore_signal(barrier, inc=1, device_id=where, device_id_type=MESH)

    greet(sibling)
    loop(1, group, lambda j: greet(device(j)))
    pl.semaphore_wait(barrier, group)

    def remote(source, target, send_sem, recv_sem, where):
        return pltpu.make_async_remote_copy(
            src_ref=source,
            dst_ref=target,
            send_sem=send_sem,
            recv_sem=recv_sem,
            device_id=where,
            device_id_type=MESH,
        )

    def landed(at, sem):
        pltpu.make_async_copy(at, at, sem).wait()

    swap = remote(low_ref.at[:, 1 - core], mate, mate_sem.at[0], mate_sem.at[1], sibling)
    swap.start()

    def up_at(block):
        return up_out.at[:, :, pl.ds(pl.multiple_of(block * size, size), size)]

    def up_copy(j):
        where = (lax.rem(chip + j, chips) * 2 + core, x)
        return remote(up_ref, up_at(seq), up_send.at[j], up_recv.at[seq], where)

    def up_forward(j):
        block = lax.rem(chip - j + chips, chips) * 2 + core
        return remote(
            up_at(block), up_at(block), up_send.at[chips + j], up_recv.at[block], sibling
        )

    up_own = remote(up_ref, up_at(seq), up_send.at[chips], up_recv.at[seq], sibling)

    def piece_copy(j):
        to, to_x = peer(j)
        part = summed.at[to, pl.ds(pl.multiple_of(to_x * rows, rows), rows), :]
        return remote(part, pieces.at[j], piece_send.at[j], piece_recv.at[j], device(j))

    def whole_at(block):
        return whole.at[pl.ds(pl.multiple_of(block * rows, rows), rows), :]

    def whole_copy(j):
        return remote(whole_at(me), whole_at(me), whole_send.at[j], whole_recv.at[me], device(j))

    def from_peer(j):
        where = device(group - j)
        return where[0] * 2 + where[1]

    def whole_forward(j):
        at = whole_at(from_peer(j))
        return remote(at, at, whole_send.at[group + j], whole_recv.at[from_peer(j)], sibling)

    swap.wait_recv()
    summed[...] = (low_ref[:, core].astype(jnp.float32) + mate[...].astype(jnp.float32)).astype(
        summed.dtype
    )
    loop(1, group, lambda j: piece_copy(j).start())
    up_own.start()
    loop(1, chips, lambda j: up_copy(j).start())
    up_out[:, :, pl.ds(pl.multiple_of(seq * size, size), size)] = up_ref[...]

    def add(j, total):
        landed(pieces.at[j], piece_recv.at[j])
        return total + pieces[j].astype(jnp.float32)

    mine = summed[chip, pl.ds(pl.multiple_of(x * rows, rows), rows), :].astype(jnp.float32)
    total = lax.fori_loop(1, group, add, mine)
    whole[pl.ds(pl.multiple_of(me * rows, rows), rows), :] = total.astype(whole.dtype)
    whole_own = remote(
        whole_at(me), whole_at(me), whole_send.at[group], whole_recv.at[me], sibling
    )
    loop(1, group, lambda j: whole_copy(j).start())
    whole_own.start()

    def pass_up(j):
        block = lax.rem(chip - j + chips, chips) * 2 + core
        landed(up_at(block), up_recv.at[block])
        up_forward(j).start()

    def pass_whole(j):
        landed(whole_at(from_peer(j)), whole_recv.at[from_peer(j)])
        whole_forward(j).start()

    loop(1, group, pass_whole)
    loop(1, chips, pass_up)

    def from_sibling(j):
        block = (j // 2 * 2 + 1 - core) * 2 + lax.rem(j, 2)
        landed(whole_at(block), whole_recv.at[block])

    loop(0, group, from_sibling)
    load.wait()
    product[...] = dot_f32(window[...], whole[...], (0, 0))
    down_out[...] = product[pl.ds(pl.multiple_of(me * own - first * 128, 8), own), :]

    def up_sibling(j):
        block = j * 2 + 1 - core
        landed(up_at(block), up_recv.at[block])

    loop(0, chips, up_sibling)
    swap.wait_send()
    up_own.wait_send()
    whole_own.wait_send()

    def sends(j):
        piece_copy(j).wait_send()
        whole_copy(j).wait_send()
        whole_forward(j).wait_send()

    def up_sends(j):
        up_copy(j).wait_send()
        up_forward(j).wait_send()

    loop(1, group, sends)
    loop(1, chips, up_sends)


def head_on_device(
    tokens,
    query_weight,
    key_weight,
    value_weight,
    adapter_down_maps,
    lifting_matrices,
    decay_logarithms,
    output_gradient,
):
    seq_count = lax.axis_size("seq")
    model_count = lax.axis_size("mp")
    length, width = tokens.shape
    heads = decay_logarithms.shape[0]
    size = query_weight.shape[1] // heads
    rank = lifting_matrices.shape[1]
    cumulative = jnp.cumsum(decay_logarithms, axis=1)
    half = jnp.bfloat16
    total_tokens = length * seq_count
    anywhere = pl.BlockSpec(memory_space=pl.ANY)
    in_vmem = pl.BlockSpec(memory_space=pltpu.VMEM)
    dma = pltpu.SemaphoreType.DMA
    layers = seq_count // 4
    token_copies = (layers - 1) * 3 + 3 + layers * 2 + 2 * layers - 1
    tokens_all, weight, upstream, cumulative = pl.pallas_call(
        exchange_kernel,
        out_shape=(
            jax.ShapeDtypeStruct((total_tokens, width), half),
            jax.ShapeDtypeStruct((width, 3 * size + 2 * rank), half),
            jax.ShapeDtypeStruct((total_tokens, size), half),
            jax.ShapeDtypeStruct((seq_count * heads, length), jnp.float32),
        ),
        in_specs=[anywhere] * 7,
        out_specs=(anywhere,) * 4,
        scratch_shapes=[
            dma((7,)),
            dma((layers + 1,)),
            dma((token_copies,)),
            dma((2 * seq_count,)),
            dma((5, seq_count)),
            dma((5, seq_count)),
        ],
        compiler_params=pltpu.CompilerParams(collective_id=0, has_side_effects=True),
    )(
        tokens,
        query_weight,
        key_weight,
        value_weight,
        adapter_down_maps,
        output_gradient,
        cumulative,
    )
    lift = lax.dynamic_slice_in_dim(lifting_matrices, lax.axis_index("seq") * size, size, 2)
    lift = (adapter_scale * lift).astype(jnp.bfloat16)
    empty = jnp.zeros_like(lift[0])
    lift = jnp.concatenate(
        [jnp.concatenate([lift[0], empty], axis=1), jnp.concatenate([empty, lift[1]], axis=1)], axis=0
    )
    low_gradient, up_products = pl.pallas_call(
        functools.partial(layer_kernel, rank),
        grid=(seq_count,),
        out_shape=(
            jax.ShapeDtypeStruct((total_tokens, 2 * rank), half),
            jax.ShapeDtypeStruct((2, rank, size), jnp.float32),
        ),
        in_specs=[
            pl.BlockSpec((length, width), lambda i: (i, 0)),
            pl.BlockSpec(weight.shape, lambda i: (0, 0)),
            pl.BlockSpec(lift.shape, lambda i: (0, 0)),
            pl.BlockSpec(cumulative.shape, lambda i: (0, 0)),
            pl.BlockSpec((length, size), lambda i: (i, 0)),
        ],
        out_specs=(
            pl.BlockSpec((total_tokens, 2 * rank), lambda i: (0, 0)),
            pl.BlockSpec((2, rank, size), lambda i: (0, 0, 0)),
        ),
        scratch_shapes=[
            pltpu.VMEM((size, size), jnp.float32),
            pltpu.VMEM((total_tokens, 2 * rank), jnp.bfloat16),
            pltpu.VMEM((total_tokens, size), jnp.bfloat16),
            pltpu.VMEM((seq_count, size, size), jnp.float32),
            pltpu.VMEM((total_tokens, 2 * size), jnp.float32),
        ],
        compiler_params=pltpu.CompilerParams(
            dimension_semantics=("arbitrary",), vmem_limit_bytes=48 * 1024 * 1024
        ),
    )(tokens_all, weight, lift, cumulative, upstream)
    count = seq_count * model_count
    own_rows = width // count
    span = 256
    grad_down, grad_up = pl.pallas_call(
        reduce_kernel,
        out_shape=(
            jax.ShapeDtypeStruct((own_rows, 2 * rank), jnp.float32),
            jax.ShapeDtypeStruct((2, rank, size * seq_count), jnp.float32),
        ),
        in_specs=[in_vmem, in_vmem, anywhere],
        out_specs=(in_vmem, in_vmem),
        scratch_shapes=[
            pltpu.VMEM((seq_count // 2, length, 2 * rank), half),
            pltpu.VMEM((seq_count // 2, length, 2 * rank), half),
            pltpu.VMEM((seq_count, length // 2, 2 * rank), half),
            pltpu.VMEM((total_tokens, 2 * rank), half),
            pltpu.VMEM((total_tokens, span), half),
            pltpu.VMEM((span, 2 * rank), jnp.float32),
            dma(()),
            dma((2,)),
            dma((seq_count,)),
            dma((seq_count,)),
            dma((count,)),
            dma((count,)),
            dma((seq_count,)),
            dma((seq_count,)),
        ],
        compiler_params=pltpu.CompilerParams(
            collective_id=1, has_side_effects=True, vmem_limit_bytes=56 * 1024 * 1024
        ),
    )(
        low_gradient.reshape(seq_count // 2, 2, length, 2 * rank), up_products, tokens_all
    )
    return (grad_down, grad_up)


def per_device(*arrays):
    length, width = arrays[0].shape
    heads = arrays[6].shape[0]
    seq_count, model_count = lax.axis_size("seq"), lax.axis_size("mp")
    size = arrays[1].shape[1] // heads
    rank = arrays[5].shape[1]
    own_rows = width // (seq_count * model_count)
    fits = (
        heads == seq_count
        and seq_count % 4 == 0
        and model_count == 2
        and length == size == 2 * rank == 128
        and arrays[1].shape[0] % 16 == 0
        and heads % 8 == 0
        and own_rows % 8 == 0
        and own_rows <= 128
        and (length // model_count) % 16 == 0
    )
    return (head_on_device if fits else on_device)(*arrays)


def solution(mesh):
    return jax.shard_map(
        per_device,
        mesh=mesh,
        in_specs=(
            P("seq", None),
            P("seq", "mp"),
            P("seq", "mp"),
            P("seq", "mp"),
            P(),
            P(None, None, "mp"),
            P("mp", "seq"),
            P("seq", "mp"),
        ),
        out_specs=(P(("seq", "mp"), None), P(None, None, "mp")),
        check_vma=False,
    )
```

```python
import functools

import jax
import jax.numpy as jnp
from jax import lax
from jax.experimental import pallas as pl
from jax.experimental.pallas import tpu as pltpu
from jax.sharding import PartitionSpec as P

adapter_scale = 2.0
eps_norm = 1e-06
exact_arithmetic = lax.Precision.HIGHEST


def carried_in(value, axis, join, neutral, backward):
    count, mine = (lax.axis_size(axis), lax.axis_index(axis))
    pieces = jax.tree.map(lambda part: lax.all_gather(part, axis), value)
    if backward:
        pieces = jax.tree.map(lambda part: part[::-1], pieces)
        mine = count - 1 - mine
    so_far = jax.tree.map(
        lambda part, zero: jnp.full_like(part, 0) + jnp.asarray(zero, part.dtype), value, neutral
    )

    def hop(position, so_far):
        longer = join(so_far, jax.tree.map(lambda part: part[position], pieces))
        return jax.tree.map(lambda new, old: jnp.where(position < mine, new, old), longer, so_far)

    return lax.fori_loop(0, count - 1, hop, so_far)


def combine(earlier, later):
    return (earlier[0] * later[0], later[0][:, None, None] * earlier[1] + later[1])


def split_heads(flat, heads):
    return flat.reshape(flat.shape[0], heads, flat.shape[1] // heads).transpose(1, 0, 2)


def join_heads(arr):
    return arr.transpose(1, 0, 2).reshape(arr.shape[1], arr.shape[0] * arr.shape[2])


def on_device(
    tokens,
    query_weight,
    key_weight,
    value_weight,
    adapter_down_maps,
    lifting_matrices,
    decay_logarithms,
    output_gradient,
):
    length = tokens.shape[0]
    heads = decay_logarithms.shape[0]
    rank_index = lifting_matrices.shape[1]
    low_product = jnp.dot(tokens, adapter_down_maps, preferred_element_type=jnp.float32).astype(
        jnp.bfloat16
    )
    query_low_product = low_product[:, :rank_index]
    value_low_product = low_product[:, rank_index:]
    cumulative = jnp.cumsum(decay_logarithms, axis=1)
    total = cumulative[:, -1]
    gain = jnp.exp(total)
    tail = jnp.exp(total[:, None] - cumulative)
    lead = jnp.exp(cumulative)
    causal = jnp.arange(length)[:, None] >= jnp.arange(length)[None, :]
    spread = cumulative[:, :, None] - cumulative[:, None, :]
    decay_mat = jnp.where(causal[None], jnp.exp(jnp.where(causal[None], spread, 0.0)), 0.0)
    pieces = (
        lax.all_gather(query_weight, "seq", axis=0, tiled=True),
        lax.all_gather(key_weight, "seq", axis=0, tiled=True),
        lax.all_gather(value_weight, "seq", axis=0, tiled=True),
    )
    columns = tokens
    query_frozen_part, key_base, value_frozen_part = tuple(
        (jnp.dot(columns, piece, preferred_element_type=jnp.float32) for piece in pieces)
    )
    value_before_norm = value_frozen_part + adapter_scale * jnp.dot(
        value_low_product, lifting_matrices[1], preferred_element_type=jnp.float32
    )
    key_heads = split_heads(jax.nn.silu(key_base).astype(jnp.bfloat16), heads)
    value_heads = split_heads(value_before_norm.astype(jnp.bfloat16), heads)
    key_f = key_heads.astype(jnp.float32)
    local = jnp.einsum(
        "hsi,hsj->hij",
        key_f * tail[:, :, None],
        value_heads.astype(jnp.float32),
        precision=exact_arithmetic,
    )
    state_in = carried_in(
        (gain, local), "seq", combine, (jnp.ones_like(gain), jnp.zeros_like(local)), False
    )[1]
    key_heads, key_f, value_heads, state_in = (key_heads, key_f, value_heads, state_in)
    query_before_norm = query_frozen_part + adapter_scale * jnp.dot(
        query_low_product, lifting_matrices[0], preferred_element_type=jnp.float32
    )
    query_heads = split_heads(jax.nn.silu(query_before_norm).astype(jnp.bfloat16), heads)
    query_f = query_heads.astype(jnp.float32)
    scores = jnp.einsum("htd,hsd->hts", query_heads, key_heads, preferred_element_type=jnp.float32)
    mixed = (scores * decay_mat).astype(jnp.bfloat16)
    attn = jnp.einsum(
        "hts,hsj->htj", mixed, value_heads, preferred_element_type=jnp.float32
    ) + lead[:, :, None] * jnp.einsum("hti,hij->htj", query_f, state_in, precision=exact_arithmetic)
    rms = jnp.sqrt(jnp.mean(attn * attn, axis=-1, keepdims=True) + eps_norm)
    normed = attn / rms
    upstream = split_heads(output_gradient, heads).astype(jnp.float32)
    d_attn = (upstream - normed * jnp.mean(upstream * normed, axis=-1, keepdims=True)) / rms
    d_attn_b = d_attn.astype(jnp.bfloat16)
    carried = jnp.einsum(
        "hti,htj->hij", query_f * lead[:, :, None], d_attn, precision=exact_arithmetic
    )
    later = carried_in(
        (gain, carried), "seq", combine, (jnp.ones_like(gain), jnp.zeros_like(carried)), True
    )[1]
    d_mixed = (
        jnp.einsum("htj,hsj->hts", d_attn_b, value_heads, preferred_element_type=jnp.float32)
        * decay_mat
    ).astype(jnp.bfloat16)
    d_query = jnp.einsum(
        "hts,hsi->hti", d_mixed, key_heads, preferred_element_type=jnp.float32
    ) + lead[:, :, None] * jnp.einsum("htj,hij->hti", d_attn, state_in, precision=exact_arithmetic)
    d_value = jnp.einsum(
        "hts,htj->hsj", mixed, d_attn_b, preferred_element_type=jnp.float32
    ) + tail[:, :, None] * jnp.einsum("hsi,hij->hsj", key_f, later, precision=exact_arithmetic)
    sig = jax.nn.sigmoid(query_before_norm)
    query_pre_gradient = join_heads(d_query) * (sig * (1.0 + query_before_norm * (1.0 - sig)))
    value_flat_gradient = join_heads(d_value)
    low_product_float = low_product.astype(jnp.float32)
    up_products = jnp.stack(
        [
            adapter_scale
            * jnp.dot(
                low_product_float[:, :rank_index].T, query_pre_gradient, precision=exact_arithmetic
            ),
            adapter_scale
            * jnp.dot(
                low_product_float[:, rank_index:].T, value_flat_gradient, precision=exact_arithmetic
            ),
        ]
    )
    grad_up = lax.psum(up_products, "seq")
    low_gradient = adapter_scale * jnp.concatenate(
        [
            jnp.dot(
                query_pre_gradient,
                lifting_matrices[0].astype(jnp.float32).T,
                precision=exact_arithmetic,
            ),
            jnp.dot(
                value_flat_gradient,
                lifting_matrices[1].astype(jnp.float32).T,
                precision=exact_arithmetic,
            ),
        ],
        axis=1,
    )
    seq_count = lax.axis_size("seq")
    model_count = lax.axis_size("mp")
    own_rows = tokens.shape[1] // (seq_count * model_count)
    whole_low = lax.psum(low_gradient, "mp")
    grouped = tokens.reshape(length, seq_count, model_count, own_rows)
    mine = lax.dynamic_index_in_dim(grouped, lax.axis_index("mp"), 2, keepdims=False).reshape(
        length, seq_count * own_rows
    )
    columns = mine.astype(jnp.float32)
    grad_down = lax.psum_scatter(
        jnp.dot(columns.T, whole_low, precision=exact_arithmetic),
        "seq",
        scatter_dimension=0,
        tiled=True,
    )
    return (grad_down, grad_up)


def dot_f32(a, b, contract):
    return lax.dot_general(a, b, ((contract[:1], contract[1:]), ((), ())), preferred_element_type=jnp.float32)


def layer_kernel(
    rank,
    tokens_ref,
    weight_ref,
    lift_ref,
    cumulative_ref,
    upstream_ref,
    low_grad_ref,
    up_ref,
    state,
    low_all,
    key_all,
    carried_all,
    grads,
):
    step = pl.program_id(0)
    steps = pl.num_programs(0)
    length = tokens_ref.shape[0]
    size = state.shape[0]
    half = jnp.bfloat16

    def decays(block):
        at = block * steps + lax.axis_index("seq")
        row = jnp.broadcast_to(cumulative_ref[pl.ds(at, 1), :], (length, length))
        column = row.T
        last = row[:, length - 1 :]
        return row, column, jnp.broadcast_to(last, (length, length))

    @pl.when(step == 0)
    def _():
        state[...] = jnp.zeros_like(state)

    product = jnp.dot(tokens_ref[...], weight_ref[...], preferred_element_type=jnp.float32)
    low = product[:, 3 * size :].astype(half)
    lifted = jnp.dot(low, lift_ref[...], preferred_element_type=jnp.float32)
    query_pre = product[:, :size] + lifted[:, :size]
    key_pre = product[:, size : 2 * size]
    value = (product[:, 2 * size : 3 * size] + lifted[:, size:]).astype(half)
    sig = jax.nn.sigmoid(query_pre)
    query = (query_pre * sig).astype(half)
    key = (key_pre * jax.nn.sigmoid(key_pre)).astype(half)
    row, column, total = decays(step)
    causal = lax.broadcasted_iota(jnp.int32, (length, length), 0) >= lax.broadcasted_iota(
        jnp.int32, (length, length), 1
    )
    decay_mat = jnp.where(causal, jnp.exp(jnp.where(causal, column - row, 0.0)), 0.0)
    lead = jnp.exp(column)
    tail = jnp.exp(total - column)
    held = state[...]
    held_half = held.astype(half)
    mixed = (dot_f32(query, key, (1, 1)) * decay_mat).astype(half)
    attn = dot_f32(mixed, value, (1, 0)) + lead * dot_f32(query, held_half, (1, 0))
    rms = jnp.sqrt(jnp.mean(attn * attn, axis=-1, keepdims=True) + eps_norm)
    normed = attn / rms
    upstream = upstream_ref[...].astype(jnp.float32)
    d_attn = (upstream - normed * jnp.mean(upstream * normed, axis=-1, keepdims=True)) / rms
    d_attn_b = d_attn.astype(half)
    carried_all[step] = dot_f32((query.astype(jnp.float32) * lead).astype(half), d_attn_b, (0, 0))
    d_mixed = (dot_f32(d_attn_b, value, (1, 1)) * decay_mat).astype(half)
    d_query = dot_f32(d_mixed, key, (1, 0)) + lead * dot_f32(d_attn_b, held_half, (1, 1))
    d_query_pre = d_query * (sig * (1.0 + query_pre * (1.0 - sig)))
    d_value = dot_f32(mixed, d_attn_b, (0, 0))
    gain = jnp.exp(total)
    state[...] = gain[:1, :] * held + dot_f32((key.astype(jnp.float32) * tail).astype(half), value, (0, 0))
    rows = pl.ds(pl.multiple_of(step * length, length), length)
    low_all[rows, :] = low
    key_all[rows, :] = key
    grads[rows, :size] = d_query_pre
    grads[rows, size:] = d_value

    @pl.when(step == steps - 1)
    def _():
        def back(i, later):
            block = steps - 1 - i
            at = pl.ds(pl.multiple_of(block * length, length), length)
            _, column, total = decays(block)
            tail = jnp.exp(total - column)
            grads[at, size:] += tail * dot_f32(key_all[at, :], later.astype(half), (1, 0))
            return carried_all[block] + jnp.exp(total)[:1, :] * later

        lax.fori_loop(0, steps, back, jnp.zeros(state.shape, jnp.float32))
        both = grads[...].astype(half)
        low_grad_ref[...] = dot_f32(both, lift_ref[...], (1, 1)).astype(half)
        ups = dot_f32(low_all[...], both, (0, 0))
        up_ref[0] = adapter_scale * ups[:rank, :size]
        up_ref[1] = adapter_scale * ups[rank:, size:]


MESH = pl.DeviceIdType.MESH


def exchange_kernel(
    tokens_ref,
    query_ref,
    key_ref,
    value_ref,
    down_ref,
    upstream_ref,
    cumulative_ref,
    tokens_all,
    weight_all,
    upstream_all,
    cumulative_all,
    local_sem,
    token_send,
    token_recv,
    block_send,
    block_recv,
):
    count = lax.axis_size("seq")
    me, x = lax.axis_index("seq"), lax.axis_index("mp")
    core, y, z = lax.rem(me, 2), lax.rem(me // 2, 2), me // 4
    layers = count // 4
    length = tokens_ref.shape[0]
    half = length // 2
    depth = query_ref.shape[0]
    size = upstream_all.shape[1]
    heads = cumulative_ref.shape[0]
    barrier = pltpu.get_barrier_semaphore()

    def greet(j, carry):
        pl.semaphore_signal(
            barrier, inc=1, device_id=(lax.rem(me + j, count), x), device_id_type=MESH
        )
        return carry

    lax.fori_loop(1, count, greet, 0)
    pl.semaphore_signal(barrier, inc=1, device_id=(me, 1 - x), device_id_type=MESH)
    pl.semaphore_wait(barrier, count)

    def seq_of(zz, yy, cc):
        return (zz * 2 + yy) * 2 + cc

    def rows_of(block, part):
        return pl.ds(pl.multiple_of(block * length + part * half, half), half)

    sent = []

    def send(block, part, device, own=False):
        source = (
            tokens_ref.at[pl.ds(pl.multiple_of(part * half, half), half), :]
            if own
            else tokens_all.at[rows_of(block, part), :]
        )
        copy = pltpu.make_async_remote_copy(
            src_ref=source,
            dst_ref=tokens_all.at[rows_of(block, part), :],
            send_sem=token_send.at[len(sent)],
            recv_sem=token_recv.at[block * 2 + part],
            device_id=device,
            device_id_type=MESH,
        )
        copy.start()
        sent.append(copy)

    def arrived(block, part):
        at = tokens_all.at[rows_of(block, part), :]
        pltpu.make_async_copy(at, at, token_recv.at[block * 2 + part]).wait()

    over_y = (seq_of(z, 1 - y, core), x)
    over_x = (me, 1 - x)
    sibling = (seq_of(z, y, 1 - core), x)
    weights = (query_ref, key_ref, value_ref)

    def block_copies(j, source, target):
        to = (target, x)
        pairs = [
            (
                weight.at[:, pl.ds(pl.multiple_of(target * size, size), size)],
                weight_all.at[
                    pl.ds(pl.multiple_of(source * depth, depth), depth), k * size : (k + 1) * size
                ],
            )
            for k, weight in enumerate(weights)
        ]
        pairs.append(
            (
                upstream_ref.at[:, pl.ds(pl.multiple_of(target * size, size), size)],
                upstream_all.at[pl.ds(pl.multiple_of(source * length, length), length), :],
            )
        )
        pairs.append(
            (
                cumulative_ref,
                cumulative_all.at[pl.ds(pl.multiple_of(source * heads, heads), heads), :],
            )
        )
        return [
            pltpu.make_async_remote_copy(
                src_ref=source_ref,
                dst_ref=dst_ref,
                send_sem=block_send.at[k, j],
                recv_sem=block_recv.at[k, j],
                device_id=to,
                device_id_type=MESH,
            )
            for k, (source_ref, dst_ref) in enumerate(pairs)
        ], pairs

    for j in range(1, layers):
        send(me, x, (seq_of(lax.rem(z + j, layers), y, core), x), own=True)
    send(me, x, over_y, own=True)
    send(me, 0, sibling, own=True)
    send(me, 1, sibling, own=True)

    def start_blocks(j, carry):
        for copy in block_copies(j, me, lax.rem(me + j, count))[0]:
            copy.start()
        return carry

    lax.fori_loop(1, count, start_blocks, 0)
    mine = [(tokens_ref, tokens_all.at[pl.ds(pl.multiple_of(me * length, length), length), :])]
    mine += block_copies(0, me, me)[1]
    mine.append((down_ref, weight_all.at[:, 3 * size :]))
    local = [
        pltpu.make_async_copy(a, b, local_sem.at[k]) for k, (a, b) in enumerate(mine)
    ]
    for copy in local:
        copy.start()

    def along_z(j):
        block = seq_of(lax.rem(z - j + layers, layers), y, core)
        arrived(block, x)
        send(block, x, over_y)
        send(block, x, over_x)
        send(block, x, sibling)

    def along_y(j):
        block = seq_of(lax.rem(z - j + layers, layers), 1 - y, core)
        arrived(block, x)
        send(block, x, over_x)
        send(block, x, sibling)

    def along_x(j):
        for other in range(2) if j else (1,):
            yy = 1 - y if other else y
            block = seq_of(lax.rem(z - j + layers, layers), yy, core)
            arrived(block, 1 - x)
            send(block, 1 - x, sibling)

    for step in range(layers + 2):
        if 1 <= step + 1 < layers:
            along_z(step + 1)
        if step < layers:
            along_y(step)
        if 0 <= step - 1 < layers:
            along_x(step - 1)
    for zz in range(layers):
        for yy in range(2):
            for part in range(2):
                arrived(seq_of(zz, yy, 1 - core), part)

    def end_blocks(j, carry):
        source = lax.rem(me - j + count, count)
        for copy in block_copies(j, source, me)[0]:
            copy.wait_recv()
        for copy in block_copies(j, me, lax.rem(me + j, count))[0]:
            copy.wait_send()
        return carry

    lax.fori_loop(1, count, end_blocks, 0)
    for copy in local:
        copy.wait()
    for copy in sent:
        copy.wait_send()


def reduce_kernel(
    low_ref,
    up_ref,
    tokens_all,
    down_out,
    up_out,
    mate,
    summed,
    pieces,
    whole,
    window,
    product,
    window_sem,
    mate_sem,
    piece_send,
    piece_recv,
    whole_send,
    whole_recv,
    up_send,
    up_recv,
):
    chips = lax.axis_size("seq") // 2
    group = chips * 2
    seq, x = lax.axis_index("seq"), lax.axis_index("mp")
    chip, core = seq // 2, lax.rem(seq, 2)
    me, place = seq * 2 + x, chip * 2 + x
    rows = pieces.shape[1]
    size = up_ref.shape[2]
    width = tokens_all.shape[1]
    own = down_out.shape[0]
    span = window.shape[1]
    sibling = (chip * 2 + 1 - core, x)
    barrier = pltpu.get_barrier_semaphore()
    first = jnp.minimum(me * own // 128, (width - span) // 128)
    load = pltpu.make_async_copy(
        tokens_all.at[:, pl.ds(pl.multiple_of(first * 128, 128), span)], window, window_sem
    )
    load.start()

    def peer(j):
        to = lax.rem(place + j, group)
        return to // 2, lax.rem(to, 2)

    def device(j):
        to, to_x = peer(j)
        return to * 2 + core, to_x

    def loop(start, stop, act):
        def body(j, carry):
            act(j)
            return carry

        lax.fori_loop(start, stop, body, 0)

    def greet(where):
        pl.semaphore_signal(barrier, inc=1, device_id=where, device_id_type=MESH)

    greet(sibling)
    loop(1, group, lambda j: greet(device(j)))
    pl.semaphore_wait(barrier, group)

    def remote(source, target, send_sem, recv_sem, where):
        return pltpu.make_async_remote_copy(
            src_ref=source,
            dst_ref=target,
            send_sem=send_sem,
            recv_sem=recv_sem,
            device_id=where,
            device_id_type=MESH,
        )

    def landed(at, sem):
        pltpu.make_async_copy(at, at, sem).wait()

    swap = remote(low_ref.at[:, 1 - core], mate, mate_sem.at[0], mate_sem.at[1], sibling)
    swap.start()

    def up_at(block):
        return up_out.at[:, :, pl.ds(pl.multiple_of(block * size, size), size)]

    def up_copy(j):
        where = (lax.rem(chip + j, chips) * 2 + core, x)
        return remote(up_ref, up_at(seq), up_send.at[j], up_recv.at[seq], where)

    def up_forward(j):
        block = lax.rem(chip - j + chips, chips) * 2 + core
        return remote(
            up_at(block), up_at(block), up_send.at[chips + j], up_recv.at[block], sibling
        )

    up_own = remote(up_ref, up_at(seq), up_send.at[chips], up_recv.at[seq], sibling)

    def piece_copy(j):
        to, to_x = peer(j)
        part = summed.at[to, pl.ds(pl.multiple_of(to_x * rows, rows), rows), :]
        return remote(part, pieces.at[j], piece_send.at[j], piece_recv.at[j], device(j))

    def whole_at(block):
        return whole.at[pl.ds(pl.multiple_of(block * rows, rows), rows), :]

    def whole_copy(j):
        return remote(whole_at(me), whole_at(me), whole_send.at[j], whole_recv.at[me], device(j))

    def from_peer(j):
        where = device(group - j)
        return where[0] * 2 + where[1]

    def whole_forward(j):
        at = whole_at(from_peer(j))
        return remote(at, at, whole_send.at[group + j], whole_recv.at[from_peer(j)], sibling)

    swap.wait_recv()
    summed[...] = (low_ref[:, core].astype(jnp.float32) + mate[...].astype(jnp.float32)).astype(
        summed.dtype
    )
    loop(1, group, lambda j: piece_copy(j).start())
    up_own.start()
    loop(1, chips, lambda j: up_copy(j).start())
    up_out[:, :, pl.ds(pl.multiple_of(seq * size, size), size)] = up_ref[...]

    def add(j, total):
        landed(pieces.at[j], piece_recv.at[j])
        return total + pieces[j].astype(jnp.float32)

    mine = summed[chip, pl.ds(pl.multiple_of(x * rows, rows), rows), :].astype(jnp.float32)
    total = lax.fori_loop(1, group, add, mine)
    whole[pl.ds(pl.multiple_of(me * rows, rows), rows), :] = total.astype(whole.dtype)
    whole_own = remote(
        whole_at(me), whole_at(me), whole_send.at[group], whole_recv.at[me], sibling
    )
    loop(1, group, lambda j: whole_copy(j).start())
    whole_own.start()

    def pass_up(j):
        block = lax.rem(chip - j + chips, chips) * 2 + core
        landed(up_at(block), up_recv.at[block])
        up_forward(j).start()

    def pass_whole(j):
        landed(whole_at(from_peer(j)), whole_recv.at[from_peer(j)])
        whole_forward(j).start()

    loop(1, group, pass_whole)
    loop(1, chips, pass_up)

    def from_sibling(j):
        block = (j // 2 * 2 + 1 - core) * 2 + lax.rem(j, 2)
        landed(whole_at(block), whole_recv.at[block])

    loop(0, group, from_sibling)
    load.wait()
    product[...] = dot_f32(window[...], whole[...], (0, 0))
    down_out[...] = product[pl.ds(pl.multiple_of(me * own - first * 128, 8), own), :]

    def up_sibling(j):
        block = j * 2 + 1 - core
        landed(up_at(block), up_recv.at[block])

    loop(0, chips, up_sibling)
    swap.wait_send()
    up_own.wait_send()
    whole_own.wait_send()

    def sends(j):
        piece_copy(j).wait_send()
        whole_copy(j).wait_send()
        whole_forward(j).wait_send()

    def up_sends(j):
        up_copy(j).wait_send()
        up_forward(j).wait_send()

    loop(1, group, sends)
    loop(1, chips, up_sends)


def head_on_device(
    tokens,
    query_weight,
    key_weight,
    value_weight,
    adapter_down_maps,
    lifting_matrices,
    decay_logarithms,
    output_gradient,
):
    seq_count = lax.axis_size("seq")
    model_count = lax.axis_size("mp")
    length, width = tokens.shape
    heads = decay_logarithms.shape[0]
    size = query_weight.shape[1] // heads
    rank = lifting_matrices.shape[1]
    cumulative = jnp.cumsum(decay_logarithms, axis=1)
    half = jnp.bfloat16
    total_tokens = length * seq_count
    anywhere = pl.BlockSpec(memory_space=pl.ANY)
    in_vmem = pl.BlockSpec(memory_space=pltpu.VMEM)
    dma = pltpu.SemaphoreType.DMA
    layers = seq_count // 4
    token_copies = (layers - 1) * 4 + 3 + layers * 2 + 2 * layers - 1
    tokens_all, weight, upstream, cumulative = pl.pallas_call(
        exchange_kernel,
        out_shape=(
            jax.ShapeDtypeStruct((total_tokens, width), half),
            jax.ShapeDtypeStruct((width, 3 * size + 2 * rank), half),
            jax.ShapeDtypeStruct((total_tokens, size), half),
            jax.ShapeDtypeStruct((seq_count * heads, length), jnp.float32),
        ),
        in_specs=[anywhere] * 7,
        out_specs=(anywhere,) * 4,
        scratch_shapes=[
            dma((7,)),
            dma((token_copies,)),
            dma((2 * seq_count,)),
            dma((5, seq_count)),
            dma((5, seq_count)),
        ],
        compiler_params=pltpu.CompilerParams(collective_id=0, has_side_effects=True),
    )(
        tokens,
        query_weight,
        key_weight,
        value_weight,
        adapter_down_maps,
        output_gradient,
        cumulative,
    )
    lift = lax.dynamic_slice_in_dim(lifting_matrices, lax.axis_index("seq") * size, size, 2)
    lift = (adapter_scale * lift).astype(jnp.bfloat16)
    empty = jnp.zeros_like(lift[0])
    lift = jnp.concatenate(
        [jnp.concatenate([lift[0], empty], axis=1), jnp.concatenate([empty, lift[1]], axis=1)], axis=0
    )
    low_gradient, up_products = pl.pallas_call(
        functools.partial(layer_kernel, rank),
        grid=(seq_count,),
        out_shape=(
            jax.ShapeDtypeStruct((total_tokens, 2 * rank), half),
            jax.ShapeDtypeStruct((2, rank, size), jnp.float32),
        ),
        in_specs=[
            pl.BlockSpec((length, width), lambda i: (i, 0)),
            pl.BlockSpec(weight.shape, lambda i: (0, 0)),
            pl.BlockSpec(lift.shape, lambda i: (0, 0)),
            pl.BlockSpec(cumulative.shape, lambda i: (0, 0)),
            pl.BlockSpec((length, size), lambda i: (i, 0)),
        ],
        out_specs=(
            pl.BlockSpec((total_tokens, 2 * rank), lambda i: (0, 0)),
            pl.BlockSpec((2, rank, size), lambda i: (0, 0, 0)),
        ),
        scratch_shapes=[
            pltpu.VMEM((size, size), jnp.float32),
            pltpu.VMEM((total_tokens, 2 * rank), jnp.bfloat16),
            pltpu.VMEM((total_tokens, size), jnp.bfloat16),
            pltpu.VMEM((seq_count, size, size), jnp.float32),
            pltpu.VMEM((total_tokens, 2 * size), jnp.float32),
        ],
        compiler_params=pltpu.CompilerParams(
            dimension_semantics=("arbitrary",), vmem_limit_bytes=48 * 1024 * 1024
        ),
    )(tokens_all, weight, lift, cumulative, upstream)
    count = seq_count * model_count
    own_rows = width // count
    span = 256
    grad_down, grad_up = pl.pallas_call(
        reduce_kernel,
        out_shape=(
            jax.ShapeDtypeStruct((own_rows, 2 * rank), jnp.float32),
            jax.ShapeDtypeStruct((2, rank, size * seq_count), jnp.float32),
        ),
        in_specs=[in_vmem, in_vmem, anywhere],
        out_specs=(in_vmem, in_vmem),
        scratch_shapes=[
            pltpu.VMEM((seq_count // 2, length, 2 * rank), half),
            pltpu.VMEM((seq_count // 2, length, 2 * rank), half),
            pltpu.VMEM((seq_count, length // 2, 2 * rank), half),
            pltpu.VMEM((total_tokens, 2 * rank), half),
            pltpu.VMEM((total_tokens, span), half),
            pltpu.VMEM((span, 2 * rank), jnp.float32),
            dma(()),
            dma((2,)),
            dma((seq_count,)),
            dma((seq_count,)),
            dma((count,)),
            dma((count,)),
            dma((seq_count,)),
            dma((seq_count,)),
        ],
        compiler_params=pltpu.CompilerParams(
            collective_id=1, has_side_effects=True, vmem_limit_bytes=56 * 1024 * 1024
        ),
    )(
        low_gradient.reshape(seq_count // 2, 2, length, 2 * rank), up_products, tokens_all
    )
    return (grad_down, grad_up)


def per_device(*arrays):
    length, width = arrays[0].shape
    heads = arrays[6].shape[0]
    seq_count, model_count = lax.axis_size("seq"), lax.axis_size("mp")
    size = arrays[1].shape[1] // heads
    rank = arrays[5].shape[1]
    own_rows = width // (seq_count * model_count)
    fits = (
        heads == seq_count
        and seq_count % 4 == 0
        and model_count == 2
        and length == size == 2 * rank == 128
        and arrays[1].shape[0] % 16 == 0
        and heads % 8 == 0
        and own_rows % 8 == 0
        and own_rows <= 128
        and (length // model_count) % 16 == 0
    )
    return (head_on_device if fits else on_device)(*arrays)


def solution(mesh):
    return jax.shard_map(
        per_device,
        mesh=mesh,
        in_specs=(
            P("seq", None),
            P("seq", "mp"),
            P("seq", "mp"),
            P("seq", "mp"),
            P(),
            P(None, None, "mp"),
            P("mp", "seq"),
            P("seq", "mp"),
        ),
        out_specs=(P(("seq", "mp"), None), P(None, None, "mp")),
        check_vma=False,
    )
```
